256 devices in a mesh: replica: 32 (over z_hi, y, core), shard: 8 (over x, z_lo).
Axes of the slice: x: 4, y: 4, z: 8 (z_hi: 4, z_lo: 2; z = z_hi * 2 + z_lo), core: 2. Of those that a mesh axis runs over, the one named last changes fastest.
Arguments:
- weight: bfloat16 [256, 8192], P(None, 'shard'), may hold values from -6 to 6
- momentum: float32 [32, 256, 8192], P('replica', None, 'shard'), may hold values from -6 to 6
- grad: bfloat16 [32, 256, 8192], P('replica', None, 'shard'), may hold values from -6 to 6
- positions: int32 [32, 4, 128, 32], P('replica', None, 'shard'), may hold values from 0 to 4095, as said below
Outputs:
- kept_state: float32 [32, 256, 8192], P('replica', None, 'shard')
- direction: bfloat16 [256, 8192], P(None, 'shard')
- new_weight: bfloat16 [256, 8192], replicated
The draws below stay inside these ranges and needn't reach their ends.
Inputs may be any that keep to these rules, and one draw needn't show every extreme that they name: The 32 positions of one block on one replica are distinct; replicas choose independently.
All inputs are finite; a program needn't handle non-finite values.
Results may differ from the reference program's by a relative error of at most 0.001.
Values may be sent and summed in bfloat16 or wider, within the bound.
No kernel may reach another device: no remote copies, remote signals or barrier semaphores. Data moves between devices by JAX's collectives and lax.ppermute only.
A program may use at most 64 MiB of HBM per device.

```python
import math
import jax
import jax.numpy as jnp
from jax import lax

D = 8192
GROUP = 64
TOPK = 32
ROWS = 256
REPLICAS = 32


def draw_positions(key, part):
    shape = (REPLICAS, ROWS // GROUP, D // GROUP, GROUP * GROUP)
    scores = jax.random.randint(key, shape, 0, 1 << 18, dtype=jnp.int32) * (GROUP * GROUP)
    scores = scores + jnp.arange(GROUP * GROUP, dtype=jnp.int32)
    chosen = lax.top_k(scores, TOPK)[1]
    return chosen.astype(jnp.int32)


def block_levels(key, extent, split, smallest, top_value):
    level, own = 1.0, jax.random.fold_in(key, 6)
    for axis_at, shards_of in split:
        heights = jnp.exp(jax.random.uniform(jax.random.fold_in(own, axis_at), (shards_of,), jnp.float32, smallest / len(split), top_value / len(split)))
        level = level * jnp.repeat(heights, extent[axis_at] // shards_of).reshape([-1 if axis == axis_at else 1 for axis in range(len(extent))])
    return level


def centred(key, dims, width, bound, split=(), kind=jnp.bfloat16):
    values = jax.random.normal(key, dims, jnp.float32) * width
    if len(split) > 0:
        values = block_levels(key, dims, split, -0.22, 0.18) * values
    return jnp.clip(values, min=-bound, max=bound).astype(kind)


def setup_inputs(seed: int = 0) -> dict:
    splits = jax.random.split(jax.random.key(seed), 5)
    return {
        "weight": centred(splits[0], (ROWS, D), 1.0, 6.0, ((1, 8),)),
        "momentum": centred(splits[1], (REPLICAS, ROWS, D), 1.0, 6.0, ((0, 32), (2, 8)), jnp.float32),
        "grad": centred(splits[2], (REPLICAS, ROWS, D), 1.0, 6.0, ((0, 32), (2, 8))),
        "positions": draw_positions(jax.random.fold_in(splits[4], 71), 0),
    }


beta_decay = 0.9
step_rate = 0.02

def dct_basis():
    freq = jnp.arange(GROUP, dtype=jnp.float32)[:, None]
    cells = jnp.arange(GROUP, dtype=jnp.float32)[None, :]
    scales = jnp.where(freq == 0, math.sqrt(1.0 / GROUP), math.sqrt(2.0 / GROUP))
    return scales * jnp.cos(math.pi * (2.0 * cells + 1.0) * freq / (2.0 * GROUP))

def reference(weight, momentum, grad, positions):
    basis_table = dct_basis()
    row_blocks = ROWS // GROUP
    col_blocks = D // GROUP
    row_index = jnp.arange(row_blocks, dtype=jnp.int32)[:, None, None]
    col_index = jnp.arange(col_blocks, dtype=jnp.int32)[None, :, None]

    def scatter_coeffs(values, where):
        flat = jnp.zeros((row_blocks, col_blocks, GROUP * GROUP), jnp.float32)
        flat = flat.at[row_index, col_index, where].add(values)
        return flat.reshape(row_blocks, col_blocks, GROUP, GROUP)

    def inverse(coeff_blocks):
        dense = jnp.einsum('ai,xyab,bj->xiyj', basis_table, coeff_blocks, basis_table, precision=lax.Precision.HIGHEST)
        return dense.reshape(ROWS, D)

    def one_replica(triple):
        state, slope, where = triple
        moved = beta_decay * state + slope.astype(jnp.float32)
        blocks = moved.reshape(row_blocks, GROUP, col_blocks, GROUP)
        coeff = jnp.einsum('ai,xiyj,bj->xyab', basis_table, blocks, basis_table, precision=lax.Precision.HIGHEST)
        coeff = coeff.reshape(row_blocks, col_blocks, GROUP * GROUP)
        picked = jnp.take_along_axis(coeff, where, axis=2)
        return (moved - inverse(scatter_coeffs(picked, where)), picked)
    kept_state, picked_all = lax.map(one_replica, (momentum, grad, positions))
    values = jnp.moveaxis(picked_all, 0, 2).reshape(row_blocks, col_blocks, REPLICAS * TOPK)
    where = jnp.moveaxis(positions, 0, 2).reshape(row_blocks, col_blocks, REPLICAS * TOPK)
    smooth = jnp.tanh(inverse(scatter_coeffs(values, where)))
    direction = smooth.astype(jnp.bfloat16)
    new_weight = (weight.astype(jnp.float32) - step_rate * smooth).astype(jnp.bfloat16)
    return (kept_state, direction, new_weight)
```

```python
import functools
import math

import jax
import jax.numpy as jnp
import numpy as np
from jax import lax
from jax.experimental import pallas as pl
from jax.experimental.pallas import tpu as pltpu
from jax.sharding import Mesh
from jax.sharding import PartitionSpec as P

GROUP = 64
REPLICA = ("zh", "y", "c")
SHARD = ("x", "zl")
beta_decay = 0.9
step_rate = 0.02
F32, BF16 = jnp.float32, jnp.bfloat16
VMEM = pl.BlockSpec(memory_space=pltpu.VMEM)
ANY = pl.BlockSpec(memory_space=pl.ANY)


def basis_parts():
    freq, cells = np.arange(GROUP)[:, None], np.arange(GROUP)[None, :]
    scales = np.where(freq == 0, math.sqrt(1.0 / GROUP), math.sqrt(2.0 / GROUP))
    table = scales * np.cos(math.pi * (2.0 * cells + 1.0) * freq / (2.0 * GROUP))
    four = np.kron(np.eye(4), table)
    high = four.astype(jnp.bfloat16)
    low = (four - high.astype(np.float64)).astype(jnp.bfloat16)
    return [np.ascontiguousarray(part) for part in (high, low, high.T, low.T)]


def two_parts(value):
    high = value.astype(BF16)
    return high, (value - high.astype(F32)).astype(BF16)


def rows_by_rows(left, right):
    return lax.dot_general(left, right, (((1,), (1,)), ((), ())), preferred_element_type=F32)


def rows_by_cols(left, right):
    return lax.dot_general(left, right, (((1,), (0,)), ((), ())), preferred_element_type=F32)


def product(dot, left, right):
    return dot(left[0], right[0]) + dot(left[0], right[1]) + dot(left[1], right[0])


def one_hot_rows(place, lines, dtype):
    line = lax.broadcasted_iota(jnp.int32, (lines, place.shape[1]), 0)
    return jnp.where(line == place, 1.0, 0.0).astype(dtype)


def split_place(flat):
    lane = lax.broadcasted_iota(jnp.int32, flat.shape, 1)
    return (flat >> 6) + ((lane >> 5) << 6), flat & 63


def spread(values, column):
    line = lax.broadcasted_iota(jnp.int32, (GROUP, values.shape[1]), 0)
    return two_parts(jnp.where(line == column, values, 0.0))


def extract_kernel(momentum, grad, positions, bh, bl, out, places):
    g = pl.program_id(0)
    mine = lax.axis_index("y")

    @pl.when(g == 0)
    def _():
        for x in range(4):
            places[:, 32 * x : 32 * x + 32] = positions[x]

    basis = (bh[...], bl[...])
    moved = beta_decay * momentum[...] + grad[...].astype(F32)
    half = product(rows_by_rows, basis, two_parts(moved))
    coeff = jnp.stack(two_parts(product(rows_by_rows, two_parts(half), basis)))
    lines = []
    for q in range(4):
        flat = places[pl.ds(4 * g + q, 1), :]
        row, column = split_place(flat)
        block = coeff[:, GROUP * q : GROUP * (q + 1)].reshape(2 * GROUP, 4 * GROUP)
        found = rows_by_cols(block, one_hot_rows(row, 4 * GROUP, BF16))
        found = found[:GROUP] + found[GROUP:]
        line = lax.broadcasted_iota(jnp.int32, found.shape, 0)
        lines.append(jnp.sum(jnp.where(line == column, found, 0.0), axis=0, keepdims=True))
        lines.append(flat.astype(F32))
    at = pl.multiple_of(8 * jnp.bitwise_xor(g, mine), 8)
    out[pl.ds(at, 8), :] = jnp.concatenate(lines, axis=0)


def extract(momentum, grad, positions, basis):
    column = lambda g: (0, g)
    whole = lambda *shape: pl.BlockSpec(shape, lambda g: (0,) * len(shape))
    return pl.pallas_call(
        extract_kernel,
        grid=(4,),
        in_specs=[
            pl.BlockSpec((256, 256), column),
            pl.BlockSpec((256, 256), column),
            whole(4, 16, 32),
            whole(256, 256),
            whole(256, 256),
        ],
        out_specs=whole(32, 128),
        out_shape=jax.ShapeDtypeStruct((32, 128), F32),
        scratch_shapes=[pltpu.VMEM((16, 128), jnp.int32)],
        cost_estimate=pl.CostEstimate(flops=10**9, bytes_accessed=2 * 2**20, transcendentals=0),
        name="extract",
    )(momentum, grad, positions, basis[0], basis[1])


def kept_kernel(momentum, grad, sent, bh, bl, th, tl, out):
    g = pl.program_id(0)
    mine = lax.axis_index("y")
    at = pl.multiple_of(8 * jnp.bitwise_xor(g, mine), 8)
    tile = sent[pl.ds(at, 8), :]
    blocks = []
    for q in range(4):
        row, column = split_place(tile[2 * q + 1 : 2 * q + 2].astype(jnp.int32))
        high, low = spread(tile[2 * q : 2 * q + 1], column)
        hot = one_hot_rows(row, 4 * GROUP, BF16)
        blocks.append(rows_by_rows(high, hot) + rows_by_rows(low, hot))
    grid = two_parts(jnp.concatenate(blocks, axis=0))
    half = product(rows_by_rows, (th[...], tl[...]), grid)
    dense = product(rows_by_cols, two_parts(half), (bh[...], bl[...]))
    moved = beta_decay * momentum[...] + grad[...].astype(F32)
    out[...] = moved - dense


def kept(momentum, grad, sent, basis):
    column = lambda g: (0, g)
    whole = lambda *shape: pl.BlockSpec(shape, lambda g: (0,) * len(shape))
    return pl.pallas_call(
        kept_kernel,
        grid=(4,),
        in_specs=[pl.BlockSpec((256, 256), column)] * 2 + [whole(32, 128)] + [whole(256, 256)] * 4,
        out_specs=pl.BlockSpec((256, 256), column),
        out_shape=jax.ShapeDtypeStruct((256, 1024), F32),
        cost_estimate=pl.CostEstimate(flops=2 * 10**9, bytes_accessed=3 * 2**20, transcendentals=0),
        name="kept",
    )(momentum, grad, sent, *basis)


def regroup_kernel(a, b, c, d, *outs):
    for k, out in enumerate(outs):
        for z, ref in enumerate((a, b, c, d)):
            out[8 * z : 8 * z + 8, :] = ref[8 * k : 8 * k + 8, :]


def regroup(arrays):
    return pl.pallas_call(
        regroup_kernel,
        in_specs=[VMEM] * 4,
        out_specs=[VMEM] * 4,
        out_shape=[jax.ShapeDtypeStruct((32, 128), F32)] * 4,
        name="regroup",
    )(*arrays)


def decode_kernel(*refs):
    entries, (weight, bh, bl, th, tl), (fresh, smooth_out, staged, sem) = refs[:8], refs[8:13], refs[13:]
    core = lax.axis_index("c")
    place = pl.multiple_of((lax.axis_index("y") * 2 + core) * 128, 128)
    copy = pltpu.make_async_copy(weight.at[:, pl.ds(place, 128)], staged, sem)
    copy.start()
    tiles = []
    for ref in entries:
        for z in range(4):
            tiles.append(jnp.where(core == 0, ref[8 * z : 8 * z + 4, :], ref[8 * z + 4 : 8 * z + 8, :]))
    blocks = []
    for j in range(2):
        total = jnp.zeros((2 * GROUP, 4 * GROUP), F32)
        for pair in range(0, len(tiles), 2):
            lefts, hots = [], []
            for tile in tiles[pair : pair + 2]:
                row, column = split_place(tile[2 * j + 1 : 2 * j + 2].astype(jnp.int32))
                lefts.append(jnp.concatenate(spread(tile[2 * j : 2 * j + 1], column), axis=0))
                hots.append(one_hot_rows(row, 4 * GROUP, BF16))
            total = total + rows_by_rows(jnp.concatenate(lefts, axis=1), jnp.concatenate(hots, axis=1))
        blocks.append(total[:GROUP] + total[GROUP:])
    grid = two_parts(jnp.concatenate(blocks, axis=0))
    half = product(rows_by_rows, (th[...], tl[...]), grid)
    dense = product(rows_by_cols, two_parts(half), (bh[:128, :128], bl[:128, :128]))
    smooth = jnp.tanh(dense)
    smooth_out[...] = smooth.astype(BF16)
    copy.wait()
    fresh[...] = (staged[...].astype(F32) - step_rate * smooth).astype(BF16)


def decode(entries, weight, basis):
    return pl.pallas_call(
        decode_kernel,
        in_specs=[VMEM] * 8 + [ANY] + [VMEM] * 4,
        out_specs=[VMEM] * 2,
        out_shape=[jax.ShapeDtypeStruct((256, 128), BF16)] * 2,
        scratch_shapes=[pltpu.VMEM((256, 128), BF16), pltpu.SemaphoreType.DMA],
        cost_estimate=pl.CostEstimate(flops=10**9, bytes_accessed=2**20, transcendentals=32768),
        name="decode",
    )(*entries, weight, *basis)


def join_kernel(*refs):
    out = refs[-1]
    at = 0
    for ref in refs[:-1]:
        size = ref.shape[0]
        out[at : at + size] = ref[...]
        at += size


def join(arrays, name):
    total = sum(array.shape[0] for array in arrays)
    return pl.pallas_call(
        join_kernel,
        in_specs=[VMEM] * len(arrays),
        out_specs=VMEM,
        out_shape=jax.ShapeDtypeStruct((total, *arrays[0].shape[1:]), arrays[0].dtype),
        name=name,
    )(*arrays)


def assemble_kernel(*refs):
    pieces, out, sem = refs[:8], refs[8], refs[9]
    core, x, y, zl = (lax.axis_index(name) for name in ("c", "x", "y", "zl"))
    copies = []
    for other in range(2):
        at_core = jnp.bitwise_xor(core, other)
        for k2 in range(4):
            for k1 in range(4):
                dx = jnp.where(at_core == 0, k1, k2)
                dy = jnp.where(at_core == 0, k2, k1)
                for dz in range(2):
                    shard = jnp.bitwise_xor(x, dx) * 2 + jnp.bitwise_xor(zl, dz)
                    tile = shard * 8 + jnp.bitwise_xor(y, dy) * 2 + at_core
                    columns = pl.ds(pl.multiple_of(tile * 128, 128), 128)
                    copy = pltpu.make_async_copy(
                        pieces[4 * other + k2].at[2 * k1 + dz], out.at[:, columns], sem.at[len(copies)]
                    )
                    copy.start()
                    copies.append(copy)
    for copy in copies:
        copy.wait()


def assemble(pieces):
    return pl.pallas_call(
        assemble_kernel,
        in_specs=[ANY] * 8,
        out_specs=ANY,
        out_shape=jax.ShapeDtypeStruct((256, 8192), BF16),
        scratch_shapes=[pltpu.SemaphoreType.DMA((64,))],
        name="assemble",
    )(*pieces)


def lay_kernel(*refs):
    pieces, out = refs[:8], refs[8]
    core, y = lax.axis_index("c"), lax.axis_index("y")
    for other in range(2):
        for k in range(4):
            tile = jnp.bitwise_xor(y, k) * 2 + jnp.bitwise_xor(core, other)
            out[:, pl.ds(pl.multiple_of(tile * 128, 128), 128)] = pieces[4 * other + k][...]


def lay(pieces):
    return pl.pallas_call(
        lay_kernel,
        in_specs=[VMEM] * 8,
        out_specs=VMEM,
        out_shape=jax.ShapeDtypeStruct((256, 1024), BF16),
        name="lay",
    )(*pieces)


def swapped(array, axis, size, k):
    return lax.ppermute(array, axis, [(i, i ^ k) for i in range(size)])


def crossed(array, first, k):
    perm = []
    for i in range(32):
        y, c, x = i >> 3, (i >> 2) & 1, i & 3
        to = (y, c, x ^ k) if c == first else (y ^ k, c, x)
        perm.append((i, (to[0] << 3) | (to[1] << 2) | to[2]))
    return lax.ppermute(array, ("y", "c", "x"), perm)


def per_device(weight, momentum, grad, positions):
    basis = [jnp.asarray(part) for part in basis_parts()]
    sent = extract(momentum[0], grad[0], positions[0], basis)
    mine = regroup([sent] + [swapped(sent, "zh", 4, k) for k in (1, 2, 3)])
    mine = [mine[0]] + [swapped(mine[k], "y", 4, k) for k in (1, 2, 3)]
    entries = mine + [swapped(part, "c", 2, 1) for part in mine]
    fresh, smooth = decode(entries, weight, basis)
    fresh = fresh[None]
    held = join([fresh, swapped(fresh, "zl", 2, 1)], "join_near")
    held = join([held] + [crossed(held, 0, k) for k in (1, 2, 3)], "join_far")
    parts = [held] + [crossed(held, 1, k) for k in (1, 2, 3)]
    new_weight = assemble(parts + [swapped(part, "c", 2, 1) for part in parts])
    smooths = [smooth] + [swapped(smooth, "y", 4, k) for k in (1, 2, 3)]
    direction = lay(smooths + [swapped(part, "c", 2, 1) for part in smooths])
    kept_state = kept(momentum[0], grad[0], sent, basis)
    return (kept_state[None], direction, new_weight)


def solution(mesh):
    split = Mesh(mesh.devices.reshape(4, 4, 2, 4, 2), ("zh", "y", "c", "x", "zl"))
    in_specs = (
        P(None, SHARD),
        P(REPLICA, None, SHARD),
        P(REPLICA, None, SHARD),
        P(REPLICA, None, SHARD, None),
    )
    out_specs = (P(REPLICA, None, SHARD), P(None, SHARD), P())
    return jax.shard_map(
        per_device, mesh=split, in_specs=in_specs, out_specs=out_specs, check_vma=False
    )
```

```python
import functools
import math

import jax
import jax.numpy as jnp
import numpy as np
from jax import lax
from jax.experimental import pallas as pl
from jax.experimental.pallas import tpu as pltpu
from jax.sharding import Mesh
from jax.sharding import PartitionSpec as P

GROUP = 64
REPLICA = ("zh", "y", "c")
SHARD = ("x", "zl")
beta_decay = 0.9
step_rate = 0.02
F32, BF16 = jnp.float32, jnp.bfloat16
VMEM = pl.BlockSpec(memory_space=pltpu.VMEM)
ANY = pl.BlockSpec(memory_space=pl.ANY)


def limit(mib):
    return pltpu.CompilerParams(vmem_limit_bytes=mib * 2**20)


def basis_parts():
    freq, cells = np.arange(GROUP)[:, None], np.arange(GROUP)[None, :]
    scales = np.where(freq == 0, math.sqrt(1.0 / GROUP), math.sqrt(2.0 / GROUP))
    table = scales * np.cos(math.pi * (2.0 * cells + 1.0) * freq / (2.0 * GROUP))
    four = np.kron(np.eye(4), table)
    high = four.astype(jnp.bfloat16)
    low = (four - high.astype(np.float64)).astype(jnp.bfloat16)
    return [np.ascontiguousarray(part) for part in (high, low, high.T, low.T)]


def two_parts(value):
    high = value.astype(BF16)
    return high, (value - high.astype(F32)).astype(BF16)


def rows_by_rows(left, right):
    return lax.dot_general(left, right, (((1,), (1,)), ((), ())), preferred_element_type=F32)


def rows_by_cols(left, right):
    return lax.dot_general(left, right, (((1,), (0,)), ((), ())), preferred_element_type=F32)


def product(dot, left, right):
    return dot(left[0], right[0]) + dot(left[0], right[1]) + dot(left[1], right[0])


def one_hot_rows(place, lines, dtype):
    line = lax.broadcasted_iota(jnp.int32, (lines, place.shape[1]), 0)
    return jnp.where(line == place, 1.0, 0.0).astype(dtype)


def split_place(flat):
    lane = lax.broadcasted_iota(jnp.int32, flat.shape, 1)
    return (flat >> 6) + ((lane >> 5) << 6), flat & 63


def spread(values, column):
    line = lax.broadcasted_iota(jnp.int32, (GROUP, values.shape[1]), 0)
    return two_parts(jnp.where(line == column, values, 0.0))


def extract_kernel(momentum, grad, positions, bh, bl, out, places):
    g = pl.program_id(0)

    @pl.when(g == 0)
    def _():
        for x in range(4):
            places[:, 32 * x : 32 * x + 32] = positions[x]

    basis = (bh[...], bl[...])
    moved = beta_decay * momentum[...] + grad[...].astype(F32)
    half = product(rows_by_rows, basis, two_parts(moved))
    coeff = jnp.stack(two_parts(product(rows_by_rows, two_parts(half), basis)))
    lines = []
    for q in range(4):
        flat = places[pl.ds(4 * g + q, 1), :]
        row, column = split_place(flat)
        block = coeff[:, GROUP * q : GROUP * (q + 1)].reshape(2 * GROUP, 4 * GROUP)
        found = rows_by_cols(block, one_hot_rows(row, 4 * GROUP, BF16))
        found = found[:GROUP] + found[GROUP:]
        line = lax.broadcasted_iota(jnp.int32, found.shape, 0)
        lines.append(jnp.sum(jnp.where(line == column, found, 0.0), axis=0, keepdims=True))
        lines.append(flat.astype(F32))
    tile = jnp.concatenate(lines, axis=0)
    for z in range(4):
        out[4 * z + g] = tile


def extract(momentum, grad, positions, basis):
    column = lambda g: (0, g)
    whole = lambda *shape: pl.BlockSpec(shape, lambda g: (0,) * len(shape))
    return pl.pallas_call(
        extract_kernel,
        grid=(4,),
        in_specs=[
            pl.BlockSpec((256, 256), column),
            pl.BlockSpec((256, 256), column),
            whole(4, 16, 32),
            whole(256, 256),
            whole(256, 256),
        ],
        out_specs=whole(16, 8, 128),
        out_shape=jax.ShapeDtypeStruct((16, 8, 128), F32),
        scratch_shapes=[pltpu.VMEM((16, 128), jnp.int32)],
        cost_estimate=pl.CostEstimate(flops=10**9, bytes_accessed=2 * 2**20, transcendentals=0),
        compiler_params=limit(12),
        name="extract",
    )(momentum, grad, positions, basis[0], basis[1])


def kept_kernel(momentum, grad, sent, bh, bl, th, tl, out):
    tile = sent[0]
    blocks = []
    for q in range(4):
        row, column = split_place(tile[2 * q + 1 : 2 * q + 2].astype(jnp.int32))
        high, low = spread(tile[2 * q : 2 * q + 1], column)
        hot = one_hot_rows(row, 4 * GROUP, BF16)
        blocks.append(rows_by_rows(high, hot) + rows_by_rows(low, hot))
    grid = two_parts(jnp.concatenate(blocks, axis=0))
    half = product(rows_by_rows, (th[...], tl[...]), grid)
    dense = product(rows_by_cols, two_parts(half), (bh[...], bl[...]))
    moved = beta_decay * momentum[...] + grad[...].astype(F32)
    out[...] = moved - dense


def kept(momentum, grad, sent, basis):
    column = lambda g: (0, g)
    whole = lambda *shape: pl.BlockSpec(shape, lambda g: (0,) * len(shape))
    return pl.pallas_call(
        kept_kernel,
        grid=(4,),
        in_specs=[pl.BlockSpec((256, 256), column)] * 2 + [pl.BlockSpec((1, 8, 128), lambda g: (g, 0, 0))] + [whole(256, 256)] * 4,
        out_specs=pl.BlockSpec((256, 256), column),
        out_shape=jax.ShapeDtypeStruct((256, 1024), F32),
        cost_estimate=pl.CostEstimate(flops=2 * 10**9, bytes_accessed=3 * 2**20, transcendentals=0),
        compiler_params=limit(12),
        name="kept",
    )(momentum, grad, sent, *basis)


def decode_kernel(*refs):
    entries, (weight, bh, bl, th, tl), (fresh, smooth_out, staged, sem) = refs[:2], refs[2:7], refs[7:]
    core = lax.axis_index("c")
    place = pl.multiple_of((lax.axis_index("y") * 2 + core) * 128, 128)
    copy = pltpu.make_async_copy(weight.at[:, pl.ds(place, 128)], staged, sem)
    copy.start()
    tiles = []
    for ref in entries:
        for source in range(16):
            tile = ref[source]
            tiles.append(jnp.where(core == 0, tile[:4], tile[4:]))
    blocks = []
    for j in range(2):
        total = jnp.zeros((2 * GROUP, 4 * GROUP), F32)
        for pair in range(0, len(tiles), 2):
            lefts, hots = [], []
            for tile in tiles[pair : pair + 2]:
                row, column = split_place(tile[2 * j + 1 : 2 * j + 2].astype(jnp.int32))
                lefts.append(jnp.concatenate(spread(tile[2 * j : 2 * j + 1], column), axis=0))
                hots.append(one_hot_rows(row, 4 * GROUP, BF16))
            total = total + rows_by_rows(jnp.concatenate(lefts, axis=1), jnp.concatenate(hots, axis=1))
        blocks.append(total[:GROUP] + total[GROUP:])
    grid = two_parts(jnp.concatenate(blocks, axis=0))
    half = product(rows_by_rows, (th[...], tl[...]), grid)
    dense = product(rows_by_cols, two_parts(half), (bh[:128, :128], bl[:128, :128]))
    smooth = jnp.tanh(dense)
    smooth_out[0] = smooth.astype(BF16)
    copy.wait()
    fresh[0] = (staged[...].astype(F32) - step_rate * smooth).astype(BF16)


def decode(entries, weight, basis):
    return pl.pallas_call(
        decode_kernel,
        in_specs=[VMEM] * 2 + [ANY] + [VMEM] * 4,
        out_specs=[VMEM] * 2,
        out_shape=[jax.ShapeDtypeStruct((1, 256, 128), BF16)] * 2,
        scratch_shapes=[pltpu.VMEM((256, 128), BF16), pltpu.SemaphoreType.DMA],
        cost_estimate=pl.CostEstimate(flops=10**9, bytes_accessed=2**20, transcendentals=32768),
        compiler_params=limit(12),
        name="decode",
    )(*entries, weight, *basis)


def join_kernel(size, *refs):
    out = refs[-1]
    for k, ref in enumerate(refs[:-1]):
        out[size * k : size * (k + 1)] = ref[:size]


def join(arrays, size, name):
    return pl.pallas_call(
        functools.partial(join_kernel, size),
        in_specs=[VMEM] * len(arrays),
        out_specs=VMEM,
        out_shape=jax.ShapeDtypeStruct((size * len(arrays), 256, 128), BF16),
        compiler_params=limit(4),
        name=name,
    )(*arrays)


def assemble_kernel(steps, *refs):
    pieces, out, sems = refs[: 2 * len(steps)], refs[-2], refs[-1]
    core, x, y, zl = (lax.axis_index(name) for name in ("c", "x", "y", "zl"))
    copies = []
    for n, k2 in enumerate(steps):
        for other in range(2):
            at_core = jnp.bitwise_xor(core, other)
            for k1 in range(4):
                dx = jnp.where(at_core == 0, k1, k2)
                dy = jnp.where(at_core == 0, k2, k1)
                for dz in range(2):
                    shard = jnp.bitwise_xor(x, dx) * 2 + jnp.bitwise_xor(zl, dz)
                    tile = shard * 8 + jnp.bitwise_xor(y, dy) * 2 + at_core
                    columns = pl.ds(pl.multiple_of(tile * 128, 128), 128)
                    copy = pltpu.make_async_copy(
                        pieces[2 * n + other].at[2 * k1 + dz], out.at[:, columns], sems.at[len(copies)]
                    )
                    copy.start()
                    copies.append(copy)
    for copy in copies:
        copy.wait()


def assemble(steps, pieces, done, name):
    before = [] if done is None else [done]
    return pl.pallas_call(
        functools.partial(assemble_kernel, steps),
        in_specs=[ANY] * (len(pieces) + len(before)),
        out_specs=ANY,
        out_shape=jax.ShapeDtypeStruct((256, 8192), BF16),
        scratch_shapes=[pltpu.SemaphoreType.DMA((16 * len(steps),))],
        input_output_aliases={} if done is None else {len(pieces): 0},
        compiler_params=limit(1),
        cost_estimate=pl.CostEstimate(flops=0, bytes_accessed=2**20 * len(steps), transcendentals=0),
        name=name,
    )(*pieces, *before)


def lay_kernel(*refs):
    pieces, out = refs[:4], refs[4]
    core, y = lax.axis_index("c"), lax.axis_index("y")
    for other in range(2):
        for k in range(4):
            tile = jnp.bitwise_xor(y, k) * 2 + jnp.bitwise_xor(core, other)
            out[:, pl.ds(pl.multiple_of(tile * 128, 128), 128)] = pieces[k][2 + other]


def lay(pieces):
    return pl.pallas_call(
        lay_kernel,
        in_specs=[VMEM] * 4,
        out_specs=VMEM,
        out_shape=jax.ShapeDtypeStruct((256, 1024), BF16),
        compiler_params=limit(4),
        name="lay",
    )(*pieces)


def choose_kernel(mine, theirs, out, sem):
    for core, source in enumerate((theirs, mine)):

        @pl.when(lax.axis_index("c") == core)
        def _():
            copy = pltpu.make_async_copy(source, out, sem)
            copy.start()
            copy.wait()


def choose(mine, theirs):
    return pl.pallas_call(
        choose_kernel,
        in_specs=[ANY] * 2,
        out_specs=ANY,
        out_shape=jax.ShapeDtypeStruct((256, 1024), BF16),
        scratch_shapes=[pltpu.SemaphoreType.DMA],
        compiler_params=limit(1),
        name="choose",
    )(mine, theirs)


def swapped(array, axis, size, k):
    return lax.ppermute(array, axis, [(i, i ^ k) for i in range(size)])


def crossed(array, first, k):
    perm = []
    for i in range(32):
        y, c, x = i >> 3, (i >> 2) & 1, i & 3
        to = (y, c, x ^ k) if c == first else (y ^ k, c, x)
        perm.append((i, (to[0] << 3) | (to[1] << 2) | to[2]))
    return lax.ppermute(array, ("y", "c", "x"), perm)


def per_device(weight, momentum, grad, positions):
    basis = [jnp.asarray(part) for part in basis_parts()]
    sent = extract(momentum[0], grad[0], positions[0], basis)
    arrived = lax.all_to_all(sent, ("zh", "y"), 0, 0, tiled=True)
    fresh, smooth = decode([arrived, swapped(arrived, "c", 2, 1)], weight, basis)
    near = [fresh, swapped(fresh, "zl", 2, 1), smooth, swapped(smooth, "c", 2, 1)]
    held = join(near, 1, "join_near")
    firsts = [held] + [crossed(held, 0, k) for k in (1, 2, 3)]
    far = join(firsts, 2, "join_far")
    parts = [far] + [crossed(far, 1, k) for k in (1, 2, 3)]
    others = [swapped(part, "c", 2, 1) for part in parts]
    laid = lay(firsts)
    direction = choose(laid, swapped(laid, "c", 2, 1))
    new_weight = assemble([0, 1], [parts[0], others[0], parts[1], others[1]], None, "assemble_a")
    new_weight = assemble([2, 3], [parts[2], others[2], parts[3], others[3]], new_weight, "assemble_b")
    kept_state = kept(momentum[0], grad[0], sent, basis)
    return (kept_state[None], direction, new_weight)


def solution(mesh):
    split = Mesh(mesh.devices.reshape(4, 4, 2, 4, 2), ("zh", "y", "c", "x", "zl"))
    in_specs = (
        P(None, SHARD),
        P(REPLICA, None, SHARD),
        P(REPLICA, None, SHARD),
        P(REPLICA, None, SHARD, None),
    )
    out_specs = (P(REPLICA, None, SHARD), P(None, SHARD), P())
    return jax.shard_map(
        per_device, mesh=split, in_specs=in_specs, out_specs=out_specs, check_vma=False
    )
```

```python
import functools
import math

import jax
import jax.numpy as jnp
import numpy as np
from jax import lax
from jax.experimental import pallas as pl
from jax.experimental.pallas import tpu as pltpu
from jax.sharding import Mesh
from jax.sharding import PartitionSpec as P

GROUP = 64
EXTRACT_MIB = 62
REPLICA = ("zh", "y", "c")
SHARD = ("x", "zl")
beta_decay = 0.9
step_rate = 0.02
F32, BF16 = jnp.float32, jnp.bfloat16
VMEM = pl.BlockSpec(memory_space=pltpu.VMEM)
ANY = pl.BlockSpec(memory_space=pl.ANY)


def limit(mib):
    return pltpu.CompilerParams(vmem_limit_bytes=mib * 2**20)


def basis_parts():
    freq, cells = np.arange(GROUP)[:, None], np.arange(GROUP)[None, :]
    scales = np.where(freq == 0, math.sqrt(1.0 / GROUP), math.sqrt(2.0 / GROUP))
    table = scales * np.cos(math.pi * (2.0 * cells + 1.0) * freq / (2.0 * GROUP))
    four = np.kron(np.eye(4), table)
    high = four.astype(jnp.bfloat16)
    low = (four - high.astype(np.float64)).astype(jnp.bfloat16)
    return np.stack([high, low, high.T, low.T])


def two_parts(value):
    high = value.astype(BF16)
    return high, (value - high.astype(F32)).astype(BF16)


def rows_by_rows(left, right):
    return lax.dot_general(left, right, (((1,), (1,)), ((), ())), preferred_element_type=F32)


def rows_by_cols(left, right):
    return lax.dot_general(left, right, (((1,), (0,)), ((), ())), preferred_element_type=F32)


def product(dot, left, right):
    return dot(left[0], right[0]) + dot(left[0], right[1]) + dot(left[1], right[0])


def one_hot_rows(place, lines, dtype):
    line = lax.broadcasted_iota(jnp.int32, (lines, place.shape[1]), 0)
    return jnp.where(line == place, 1.0, 0.0).astype(dtype)


def split_place(flat):
    lane = lax.broadcasted_iota(jnp.int32, flat.shape, 1)
    return (flat >> 6) + ((lane >> 5) << 6), flat & 63


def spread(values, column):
    line = lax.broadcasted_iota(jnp.int32, (GROUP, values.shape[1]), 0)
    return two_parts(jnp.where(line == column, values, 0.0))


def extract_kernel(momentum, grad, positions, weight, table, out, column, basis, places, sems):
    g = pl.program_id(0)
    place = pl.multiple_of((lax.axis_index("y") * 2 + lax.axis_index("c")) * 128, 128)
    copies = [
        pltpu.make_async_copy(weight.at[:, pl.ds(place, 128)], column, sems.at[0]),
        pltpu.make_async_copy(table, basis, sems.at[1]),
    ]

    @pl.when(g == 0)
    def _():
        for copy in copies[::-1]:
            copy.start()
        for x in range(4):
            places[:, 32 * x : 32 * x + 32] = positions[x]
        copies[1].wait()

    straight = (basis[0], basis[1])
    moved = beta_decay * momentum[...] + grad[...].astype(F32)
    half = product(rows_by_rows, straight, two_parts(moved))
    coeff = jnp.stack(two_parts(product(rows_by_rows, two_parts(half), straight)))
    lines = []
    for q in range(4):
        flat = places[pl.ds(4 * g + q, 1), :]
        row, column = split_place(flat)
        block = coeff[:, GROUP * q : GROUP * (q + 1)].reshape(2 * GROUP, 4 * GROUP)
        found = rows_by_cols(block, one_hot_rows(row, 4 * GROUP, BF16))
        found = found[:GROUP] + found[GROUP:]
        line = lax.broadcasted_iota(jnp.int32, found.shape, 0)
        lines.append(jnp.sum(jnp.where(line == column, found, 0.0), axis=0, keepdims=True))
        lines.append(flat.astype(F32))
    tile = jnp.concatenate(lines, axis=0)
    for z in range(4):
        out[4 * z + g] = tile

    @pl.when(g == 3)
    def _():
        copies[0].wait()


def extract(momentum, grad, positions, weight, table):
    block = pl.BlockSpec((256, 256), lambda g: (0, g))
    whole = lambda *shape: pl.BlockSpec(shape, lambda g: (0,) * len(shape))
    return pl.pallas_call(
        extract_kernel,
        grid=(4,),
        in_specs=[block, block, whole(4, 16, 32), ANY, ANY],
        out_specs=[whole(16, 8, 128), VMEM, VMEM],
        out_shape=[
            jax.ShapeDtypeStruct((16, 8, 128), F32),
            jax.ShapeDtypeStruct((256, 128), BF16),
            jax.ShapeDtypeStruct((4, 256, 256), BF16),
        ],
        scratch_shapes=[pltpu.VMEM((16, 128), jnp.int32), pltpu.SemaphoreType.DMA((2,))],
        cost_estimate=pl.CostEstimate(flops=10**9, bytes_accessed=2 * 2**20, transcendentals=0),
        compiler_params=limit(EXTRACT_MIB),
        name="extract",
    )(momentum, grad, positions, weight, table)


def kept_kernel(momentum, grad, sent, basis, *refs):
    g = pl.program_id(0)
    pieces, out, laid = refs[:4], refs[4], refs[5]
    core, y = lax.axis_index("c"), lax.axis_index("y")
    for k in range(4):

        @pl.when(g == k)
        def _():
            for other in range(2):
                tile = jnp.bitwise_xor(y, k) * 2 + jnp.bitwise_xor(core, other)
                laid[:, pl.ds(pl.multiple_of(tile * 128, 128), 128)] = pieces[k][2 + other]

    tile = sent[0]
    blocks = []
    for q in range(4):
        row, column = split_place(tile[2 * q + 1 : 2 * q + 2].astype(jnp.int32))
        high, low = spread(tile[2 * q : 2 * q + 1], column)
        hot = one_hot_rows(row, 4 * GROUP, BF16)
        blocks.append(rows_by_rows(high, hot) + rows_by_rows(low, hot))
    grid = two_parts(jnp.concatenate(blocks, axis=0))
    half = product(rows_by_rows, (basis[2], basis[3]), grid)
    dense = product(rows_by_cols, two_parts(half), (basis[0], basis[1]))
    moved = beta_decay * momentum[...] + grad[...].astype(F32)
    out[...] = moved - dense


def kept(momentum, grad, sent, basis, pieces):
    block = pl.BlockSpec((256, 256), lambda g: (0, g))
    whole = lambda *shape: pl.BlockSpec(shape, lambda g: (0,) * len(shape))
    return pl.pallas_call(
        kept_kernel,
        grid=(4,),
        in_specs=[block, block, pl.BlockSpec((1, 8, 128), lambda g: (g, 0, 0)), VMEM] + [VMEM] * 4,
        out_specs=[block, VMEM],
        out_shape=[jax.ShapeDtypeStruct((256, 1024), F32), jax.ShapeDtypeStruct((256, 1024), BF16)],
        cost_estimate=pl.CostEstimate(flops=2 * 10**9, bytes_accessed=3 * 2**20, transcendentals=0),
        compiler_params=limit(12),
        name="kept",
    )(momentum, grad, sent, basis, *pieces)


def decode_kernel(*refs):
    entries, (column, basis, fresh, smooth_out) = refs[:2], refs[2:]
    core = lax.axis_index("c")
    tiles = []
    for ref in entries:
        for source in range(16):
            tile = ref[source]
            tiles.append(jnp.where(core == 0, tile[:4], tile[4:]))
    blocks = []
    for j in range(2):
        total = jnp.zeros((2 * GROUP, 4 * GROUP), F32)
        for pair in range(0, len(tiles), 2):
            lefts, hots = [], []
            for tile in tiles[pair : pair + 2]:
                row, line = split_place(tile[2 * j + 1 : 2 * j + 2].astype(jnp.int32))
                lefts.append(jnp.concatenate(spread(tile[2 * j : 2 * j + 1], line), axis=0))
                hots.append(one_hot_rows(row, 4 * GROUP, BF16))
            total = total + rows_by_rows(jnp.concatenate(lefts, axis=1), jnp.concatenate(hots, axis=1))
        blocks.append(total[:GROUP] + total[GROUP:])
    grid = two_parts(jnp.concatenate(blocks, axis=0))
    half = product(rows_by_rows, (basis[2], basis[3]), grid)
    dense = product(rows_by_cols, two_parts(half), (basis[0, :128, :128], basis[1, :128, :128]))
    smooth = jnp.tanh(dense)
    smooth_out[0] = smooth.astype(BF16)
    fresh[0] = (column[...].astype(F32) - step_rate * smooth).astype(BF16)


def decode(entries, column, basis):
    return pl.pallas_call(
        decode_kernel,
        in_specs=[VMEM] * 4,
        out_specs=[VMEM] * 2,
        out_shape=[jax.ShapeDtypeStruct((1, 256, 128), BF16)] * 2,
        cost_estimate=pl.CostEstimate(flops=10**9, bytes_accessed=2**20, transcendentals=32768),
        compiler_params=limit(12),
        name="decode",
    )(*entries, column, basis)


def join_kernel(size, *refs):
    out = refs[-1]
    for k, ref in enumerate(refs[:-1]):
        out[size * k : size * (k + 1)] = ref[:size]


def join(arrays, size, name):
    return pl.pallas_call(
        functools.partial(join_kernel, size),
        in_specs=[VMEM] * len(arrays),
        out_specs=VMEM,
        out_shape=jax.ShapeDtypeStruct((size * len(arrays), 256, 128), BF16),
        compiler_params=limit(4),
        name=name,
    )(*arrays)


def assemble_kernel(steps, *refs):
    pieces, out, sems = refs[: 2 * len(steps)], refs[-2], refs[-1]
    core, x, y, zl = (lax.axis_index(name) for name in ("c", "x", "y", "zl"))
    copies = []
    for n, k2 in enumerate(steps):
        for other in range(2):
            at_core = jnp.bitwise_xor(core, other)
            for k1 in range(4):
                dx = jnp.where(at_core == 0, k1, k2)
                dy = jnp.where(at_core == 0, k2, k1)
                for dz in range(2):
                    shard = jnp.bitwise_xor(x, dx) * 2 + jnp.bitwise_xor(zl, dz)
                    tile = shard * 8 + jnp.bitwise_xor(y, dy) * 2 + at_core
                    columns = pl.ds(pl.multiple_of(tile * 128, 128), 128)
                    copy = pltpu.make_async_copy(
                        pieces[2 * n + other].at[2 * k1 + dz], out.at[:, columns], sems.at[len(copies)]
                    )
                    copy.start()
                    copies.append(copy)
    for copy in copies:
        copy.wait()


def assemble(steps, pieces, done, name):
    before = [] if done is None else [done]
    return pl.pallas_call(
        functools.partial(assemble_kernel, steps),
        in_specs=[ANY] * (len(pieces) + len(before)),
        out_specs=ANY,
        out_shape=jax.ShapeDtypeStruct((256, 8192), BF16),
        scratch_shapes=[pltpu.SemaphoreType.DMA((16 * len(steps),))],
        input_output_aliases={} if done is None else {len(pieces): 0},
        compiler_params=limit(1),
        cost_estimate=pl.CostEstimate(flops=0, bytes_accessed=2**20 * len(steps), transcendentals=0),
        name=name,
    )(*pieces, *before)


def choose_kernel(mine, theirs, out, sem):
    for core, source in enumerate((theirs, mine)):

        @pl.when(lax.axis_index("c") == core)
        def _():
            copy = pltpu.make_async_copy(source, out, sem)
            copy.start()
            copy.wait()


def choose(mine, theirs):
    return pl.pallas_call(
        choose_kernel,
        in_specs=[ANY] * 2,
        out_specs=ANY,
        out_shape=jax.ShapeDtypeStruct((256, 1024), BF16),
        scratch_shapes=[pltpu.SemaphoreType.DMA],
        compiler_params=limit(1),
        name="choose",
    )(mine, theirs)


def swapped(array, axis, size, k):
    return lax.ppermute(array, axis, [(i, i ^ k) for i in range(size)])


def crossed(array, first, k):
    perm = []
    for i in range(32):
        y, c, x = i >> 3, (i >> 2) & 1, i & 3
        to = (y, c, x ^ k) if c == first else (y ^ k, c, x)
        perm.append((i, (to[0] << 3) | (to[1] << 2) | to[2]))
    return lax.ppermute(array, ("y", "c", "x"), perm)


def per_device(weight, momentum, grad, positions):
    table = jnp.asarray(basis_parts())
    sent, column, basis = extract(momentum[0], grad[0], positions[0], weight, table)
    arrived = lax.all_to_all(sent, ("zh", "y"), 0, 0, tiled=True)
    fresh, smooth = decode([arrived, swapped(arrived, "c", 2, 1)], column, basis)
    near = [fresh, swapped(fresh, "zl", 2, 1), smooth, swapped(smooth, "c", 2, 1)]
    held = join(near, 1, "join_near")
    firsts = [held] + [crossed(held, 0, k) for k in (1, 2, 3)]
    far = join(firsts, 2, "join_far")
    parts = [far] + [crossed(far, 1, k) for k in (1, 2, 3)]
    others = [swapped(part, "c", 2, 1) for part in parts]
    kept_state, laid = kept(momentum[0], grad[0], sent, basis, firsts)
    direction = choose(laid, swapped(laid, "c", 2, 1))
    new_weight = assemble([0, 1], [parts[0], others[0], parts[1], others[1]], None, "assemble_a")
    new_weight = assemble([2, 3], [parts[2], others[2], parts[3], others[3]], new_weight, "assemble_b")
    return (kept_state[None], direction, new_weight)


def solution(mesh):
    split = Mesh(mesh.devices.reshape(4, 4, 2, 4, 2), ("zh", "y", "c", "x", "zl"))
    in_specs = (
        P(None, SHARD),
        P(REPLICA, None, SHARD),
        P(REPLICA, None, SHARD),
        P(REPLICA, None, SHARD, None),
    )
    out_specs = (P(REPLICA, None, SHARD), P(None, SHARD), P())
    return jax.shard_map(
        per_device, mesh=split, in_specs=in_specs, out_specs=out_specs, check_vma=False
    )
```

```python
import functools
import math

import jax
import jax.numpy as jnp
import numpy as np
from jax import lax
from jax.experimental import pallas as pl
from jax.experimental.pallas import tpu as pltpu
from jax.sharding import Mesh
from jax.sharding import PartitionSpec as P

GROUP = 64
REPLICA = ("zh", "y", "c")
SHARD = ("x", "zl")
beta_decay = 0.9
step_rate = 0.02
F32, BF16 = jnp.float32, jnp.bfloat16
VMEM = pl.BlockSpec(memory_space=pltpu.VMEM)
ANY = pl.BlockSpec(memory_space=pl.ANY)
HBM = pl.BlockSpec(memory_space=pltpu.HBM)


def limit(mib):
    return pltpu.CompilerParams(vmem_limit_bytes=int(mib * 2**20))


def basis_parts():
    freq, cells = np.arange(GROUP)[:, None], np.arange(GROUP)[None, :]
    scales = np.where(freq == 0, math.sqrt(1.0 / GROUP), math.sqrt(2.0 / GROUP))
    table = scales * np.cos(math.pi * (2.0 * cells + 1.0) * freq / (2.0 * GROUP))
    four = np.kron(np.eye(4), table)
    high = four.astype(jnp.bfloat16)
    low = (four - high.astype(np.float64)).astype(jnp.bfloat16)
    return np.stack([high, low, high.T, low.T])


def two_parts(value):
    high = value.astype(BF16)
    return high, (value - high.astype(F32)).astype(BF16)


def rows_by_rows(left, right):
    return lax.dot_general(left, right, (((1,), (1,)), ((), ())), preferred_element_type=F32)


def rows_by_cols(left, right):
    return lax.dot_general(left, right, (((1,), (0,)), ((), ())), preferred_element_type=F32)


def product(dot, left, right):
    return dot(left[0], right[0]) + dot(left[0], right[1]) + dot(left[1], right[0])


def one_hot_rows(place, lines, dtype):
    line = lax.broadcasted_iota(jnp.int32, (lines, place.shape[1]), 0)
    return jnp.where(line == place, 1.0, 0.0).astype(dtype)


def split_place(flat):
    lane = lax.broadcasted_iota(jnp.int32, flat.shape, 1)
    return (flat >> 6) + ((lane >> 5) << 6), flat & 63


def spread(values, column):
    line = lax.broadcasted_iota(jnp.int32, (GROUP, values.shape[1]), 0)
    return two_parts(jnp.where(line == column, values, 0.0))


def extract_kernel(momentum, grad, positions, table, out, m_in, g_in, p_in, basis, places, sems):
    copies = []
    for half in range(2):
        columns = pl.ds(512 * half, 512)
        copies.append((momentum.at[:, columns], m_in.at[half]))
        copies.append((grad.at[:, columns], g_in.at[half]))
        if half == 0:
            copies.append((table.at[pl.ds(0, 2)], basis))
            copies.append((positions, p_in))
    copies = [pltpu.make_async_copy(*pair, sems.at[n]) for n, pair in enumerate(copies)]
    for copy in copies:
        copy.start()
    for half in range(2):
        for copy in copies[4:] if half else copies[:4]:
            copy.wait()
        if half == 0:
            for x in range(4):
                places[:, 32 * x : 32 * x + 32] = p_in[x]
        straight = (basis[0], basis[1])
        moved = beta_decay * m_in[half] + g_in[half].astype(F32)
        moved = [two_parts(moved[:, 256 * g : 256 * g + 256]) for g in range(2)]
        rows = [two_parts(product(rows_by_rows, straight, value)) for value in moved]
        coeff = [two_parts(product(rows_by_rows, value, straight)) for value in rows]
        for g in range(2):
            lines = []
            for q in range(4):
                at = 8 * half + 4 * g + q
                flat = places[at : at + 1, :]
                row, column = split_place(flat)
                block = jnp.concatenate([part[GROUP * q : GROUP * (q + 1)] for part in coeff[g]], axis=0)
                found = rows_by_cols(block, one_hot_rows(row, 4 * GROUP, BF16))
                found = found[:GROUP] + found[GROUP:]
                line = lax.broadcasted_iota(jnp.int32, found.shape, 0)
                lines.append(jnp.sum(jnp.where(line == column, found, 0.0), axis=0, keepdims=True))
                lines.append(flat.astype(F32))
            tile = jnp.concatenate(lines, axis=0)
            for z in range(4):
                out[4 * z + 2 * half + g] = tile


def extract(momentum, grad, positions, table):
    return pl.pallas_call(
        extract_kernel,
        in_specs=[HBM] * 4,
        out_specs=VMEM,
        out_shape=jax.ShapeDtypeStruct((16, 8, 128), F32),
        scratch_shapes=[
            pltpu.VMEM((2, 256, 512), F32),
            pltpu.VMEM((2, 256, 512), BF16),
            pltpu.VMEM((4, 16, 32), jnp.int32),
            pltpu.VMEM((2, 256, 256), BF16),
            pltpu.VMEM((16, 128), jnp.int32),
            pltpu.SemaphoreType.DMA((6,)),
        ],
        cost_estimate=pl.CostEstimate(flops=10**9, bytes_accessed=2 * 2**20, transcendentals=0),
        compiler_params=limit(59),
        name="extract",
    )(momentum, grad, positions, table)


def kept_kernel(momentum, grad, sent, basis, out, token):
    straight, turned = (basis[0], basis[1]), (basis[2], basis[3])
    grids = []
    for g in range(2):
        tile, blocks = sent[g], []
        for q in range(4):
            row, column = split_place(tile[2 * q + 1 : 2 * q + 2].astype(jnp.int32))
            high, low = spread(tile[2 * q : 2 * q + 1], column)
            hot = one_hot_rows(row, 4 * GROUP, BF16)
            blocks.append(rows_by_rows(high, hot) + rows_by_rows(low, hot))
        grids.append(two_parts(jnp.concatenate(blocks, axis=0)))
    half = [two_parts(product(rows_by_rows, turned, grid)) for grid in grids]
    dense = [product(rows_by_cols, value, straight) for value in half]
    moved = beta_decay * momentum[...] + grad[...].astype(F32)
    for g in range(2):
        columns = slice(256 * g, 256 * g + 256)
        out[:, columns] = moved[:, columns] - dense[g]
    token[...] = jnp.zeros_like(token)


def kept(momentum, grad, sent, table):
    block = pl.BlockSpec((256, 512), lambda g: (0, g))
    whole = lambda *shape: pl.BlockSpec(shape, lambda g: (0,) * len(shape))
    return pl.pallas_call(
        kept_kernel,
        grid=(2,),
        in_specs=[block, block, pl.BlockSpec((2, 8, 128), lambda g: (g, 0, 0)), whole(4, 256, 256)],
        out_specs=[block, whole(8, 128)],
        out_shape=[jax.ShapeDtypeStruct((256, 1024), F32), jax.ShapeDtypeStruct((8, 128), F32)],
        cost_estimate=pl.CostEstimate(flops=2 * 10**9, bytes_accessed=3 * 2**20, transcendentals=0),
        compiler_params=limit(12),
        name="kept",
    )(momentum, grad, sent, table)


def decode_kernel(*refs):
    entries, (weight, basis, fresh, smooth_out) = refs[:2], refs[2:]
    core = lax.axis_index("c")
    place = pl.multiple_of((lax.axis_index("y") * 2 + core) * 128, 128)
    tiles = []
    for ref in entries:
        for source in range(16):
            tile = ref[source]
            tiles.append(jnp.where(core == 0, tile[:4], tile[4:]))
    totals = [jnp.zeros((2 * GROUP, 4 * GROUP), F32)] * 2
    for pair in range(0, len(tiles), 2):
        for j in range(2):
            lefts, hots = [], []
            for tile in tiles[pair : pair + 2]:
                row, line = split_place(tile[2 * j + 1 : 2 * j + 2].astype(jnp.int32))
                lefts.append(jnp.concatenate(spread(tile[2 * j : 2 * j + 1], line), axis=0))
                hots.append(one_hot_rows(row, 4 * GROUP, BF16))
            found = rows_by_rows(jnp.concatenate(lefts, axis=1), jnp.concatenate(hots, axis=1))
            totals[j] = totals[j] + found
    blocks = [total[:GROUP] + total[GROUP:] for total in totals]
    grid = two_parts(jnp.concatenate(blocks, axis=0))
    half = product(rows_by_rows, (basis[2], basis[3]), grid)
    dense = product(rows_by_cols, two_parts(half), (basis[0, :128, :128], basis[1, :128, :128]))
    smooth = jnp.tanh(dense)
    smooth_out[0] = smooth.astype(BF16)
    fresh[0] = (weight[:, pl.ds(place, 128)].astype(F32) - step_rate * smooth).astype(BF16)


def decode(entries, weight, table):
    return pl.pallas_call(
        decode_kernel,
        in_specs=[VMEM] * 4,
        out_specs=[VMEM] * 2,
        out_shape=[jax.ShapeDtypeStruct((1, 256, 128), BF16)] * 2,
        cost_estimate=pl.CostEstimate(flops=10**9, bytes_accessed=2**20, transcendentals=32768),
        compiler_params=limit(12),
        name="decode",
    )(*entries, weight, table)


def near_kernel(a, b, c, d, out):
    for k, ref in enumerate((a, b, c, d)):
        out[k] = ref[0]


def join_near(arrays):
    return pl.pallas_call(
        near_kernel,
        in_specs=[VMEM] * 4,
        out_specs=VMEM,
        out_shape=jax.ShapeDtypeStruct((4, 256, 128), BF16),
        compiler_params=limit(4),
        name="join_near",
    )(*arrays)


def own_kernel(a, b, c, d, token, out):
    for k, ref in enumerate((a, b, c, d)):
        out[k] = ref[0]


def join_own(arrays, token):
    return pl.pallas_call(
        own_kernel,
        in_specs=[VMEM] * 4 + [ANY],
        out_specs=VMEM,
        out_shape=jax.ShapeDtypeStruct((4, 256, 128), BF16),
        compiler_params=limit(4),
        name="join_own",
    )(*arrays, token)


def far_kernel(own, a, b, c, d, out):
    out[:4] = own[...]
    for k, ref in enumerate((a, b, c, d)):
        out[4 + k] = ref[1]


def join_far(own, arrays):
    return pl.pallas_call(
        far_kernel,
        in_specs=[VMEM] * 5,
        out_specs=VMEM,
        out_shape=jax.ShapeDtypeStruct((8, 256, 128), BF16),
        compiler_params=limit(4),
        name="join_far",
    )(own, *arrays)


def piece_copies(groups, pieces, out, sems):
    core, x, y, zl = (lax.axis_index(name) for name in ("c", "x", "y", "zl"))
    copies = []
    for n, (k2, zs) in enumerate(groups):
        for other in range(2):
            at_core = jnp.bitwise_xor(core, other)
            for i, dz in enumerate(zs):
                for k1 in range(4):
                    dx = jnp.where(at_core == 0, k1, k2)
                    dy = jnp.where(at_core == 0, k2, k1)
                    shard = jnp.bitwise_xor(x, dx) * 2 + jnp.bitwise_xor(zl, dz)
                    tile = shard * 8 + jnp.bitwise_xor(y, dy) * 2 + at_core
                    columns = pl.ds(pl.multiple_of(tile * 128, 128), 128)
                    copies.append(
                        pltpu.make_async_copy(
                            pieces[2 * n + other].at[4 * i + k1], out.at[:, columns], sems.at[len(copies)]
                        )
                    )
    return copies


def count_copies(groups):
    return sum(8 * len(zs) for _, zs in groups)


NEW_WEIGHT = jax.ShapeDtypeStruct((256, 8192), BF16)
LAID = jax.ShapeDtypeStruct((256, 1024), BF16)


def lay_kernel(groups, *refs):
    firsts, pieces, (laid, out, sems) = refs[:4], refs[4:-3], refs[-3:]
    copies = piece_copies(groups, pieces, out, sems)
    for copy in copies:
        copy.start()
    core, y = lax.axis_index("c"), lax.axis_index("y")
    for k in range(4):
        for other in range(2):
            tile = jnp.bitwise_xor(y, k) * 2 + jnp.bitwise_xor(core, other)
            laid[:, pl.ds(pl.multiple_of(tile * 128, 128), 128)] = firsts[k][2 + other]
    for copy in copies:
        copy.wait()


def lay(firsts, groups, pieces):
    return pl.pallas_call(
        functools.partial(lay_kernel, groups),
        in_specs=[VMEM] * 4 + [ANY] * len(pieces),
        out_specs=[VMEM, ANY],
        out_shape=[LAID, NEW_WEIGHT],
        scratch_shapes=[pltpu.SemaphoreType.DMA((count_copies(groups),))],
        compiler_params=limit(4),
        name="lay",
    )(*firsts, *pieces)


def choose_kernel(groups, mine, theirs, *refs):
    pieces, (direction, out, sems, sem) = refs[: 2 * len(groups)], refs[-4:]
    copies = piece_copies(groups, pieces, out, sems)
    for copy in copies:
        copy.start()
    for core, source in enumerate((theirs, mine)):

        @pl.when(lax.axis_index("c") == core)
        def _():
            copy = pltpu.make_async_copy(source, direction, sem)
            copy.start()
            copy.wait()

    for copy in copies:
        copy.wait()


def choose(mine, theirs, groups, pieces, done):
    return pl.pallas_call(
        functools.partial(choose_kernel, groups),
        in_specs=[ANY] * (3 + len(pieces)),
        out_specs=[ANY] * 2,
        out_shape=[LAID, NEW_WEIGHT],
        scratch_shapes=[pltpu.SemaphoreType.DMA((count_copies(groups),)), pltpu.SemaphoreType.DMA],
        input_output_aliases={2 + len(pieces): 1},
        compiler_params=limit(1),
        name="choose",
    )(mine, theirs, *pieces, done)


def finish_kernel(groups, *refs):
    pieces, (out, sems) = refs[: 2 * len(groups)], refs[-2:]
    copies = piece_copies(groups, pieces, out, sems)
    for copy in copies:
        copy.start()
    for copy in copies:
        copy.wait()


def finish(groups, pieces, done):
    return pl.pallas_call(
        functools.partial(finish_kernel, groups),
        in_specs=[ANY] * (1 + len(pieces)),
        out_specs=ANY,
        out_shape=NEW_WEIGHT,
        scratch_shapes=[pltpu.SemaphoreType.DMA((count_copies(groups),))],
        input_output_aliases={len(pieces): 0},
        compiler_params=limit(1),
        name="finish",
    )(*pieces, done)


def swapped(array, axis, size, k):
    return lax.ppermute(array, axis, [(i, i ^ k) for i in range(size)])


def crossed(array, first, k):
    perm = []
    for i in range(32):
        y, c, x = i >> 3, (i >> 2) & 1, i & 3
        to = (y, c, x ^ k) if c == first else (y ^ k, c, x)
        perm.append((i, (to[0] << 3) | (to[1] << 2) | to[2]))
    return lax.ppermute(array, ("y", "c", "x"), perm)


def other_core(array):
    return swapped(array, "c", 2, 1)


def per_device(weight, momentum, grad, positions):
    table = jnp.asarray(basis_parts())
    sent = extract(momentum[0], grad[0], positions[0], table)
    arrived = lax.all_to_all(sent, ("zh", "y"), 0, 0, tiled=True)
    fresh, smooth = decode([arrived, other_core(arrived)], other_core(weight), other_core(table))
    near = join_near([fresh, swapped(fresh, "zl", 2, 1), smooth, other_core(smooth)])
    firsts = [near] + [crossed(near, 0, k) for k in (1, 2, 3)]
    kept_state, token = kept(momentum[0], grad[0], sent, table)
    own = join_own(firsts, token)
    two = crossed(own, 1, 2)
    far = join_far(own, firsts)
    one, three = crossed(far, 1, 1), crossed(far, 1, 3)
    two_z = swapped(two, "zl", 2, 1)
    both = lambda array: [array, other_core(array)]
    laid, new_weight = lay(firsts, [(0, (0, 1))], both(far))
    direction, new_weight = choose(
        laid,
        other_core(laid),
        [(1, (0, 1)), (2, (0,)), (2, (1,))],
        both(one) + both(two) + both(two_z),
        new_weight,
    )
    new_weight = finish([(3, (0, 1))], both(three), new_weight)
    return (kept_state[None], direction, new_weight)


def solution(mesh):
    split = Mesh(mesh.devices.reshape(4, 4, 2, 4, 2), ("zh", "y", "c", "x", "zl"))
    in_specs = (
        P(None, SHARD),
        P(REPLICA, None, SHARD),
        P(REPLICA, None, SHARD),
        P(REPLICA, None, SHARD, None),
    )
    out_specs = (P(REPLICA, None, SHARD), P(None, SHARD), P())
    return jax.shard_map(
        per_device, mesh=split, in_specs=in_specs, out_specs=out_specs, check_vma=False
    )
```

```python
import functools
import math

import jax
import jax.numpy as jnp
import numpy as np
from jax import lax
from jax.experimental import pallas as pl
from jax.experimental.pallas import tpu as pltpu
from jax.sharding import Mesh
from jax.sharding import PartitionSpec as P

GROUP = 64
REPLICA = ("zh", "y", "c")
SHARD = ("x", "zl")
beta_decay = 0.9
step_rate = 0.02
F32, BF16 = jnp.float32, jnp.bfloat16
VMEM = pl.BlockSpec(memory_space=pltpu.VMEM)
RING = (1, 3, 2)
ANY = pl.BlockSpec(memory_space=pl.ANY)
HBM = pl.BlockSpec(memory_space=pltpu.HBM)


def limit(mib):
    return pltpu.CompilerParams(vmem_limit_bytes=int(mib * 2**20))


def basis_parts():
    freq, cells = np.arange(GROUP)[:, None], np.arange(GROUP)[None, :]
    scales = np.where(freq == 0, math.sqrt(1.0 / GROUP), math.sqrt(2.0 / GROUP))
    table = scales * np.cos(math.pi * (2.0 * cells + 1.0) * freq / (2.0 * GROUP))
    four = np.kron(np.eye(4), table)
    high = four.astype(jnp.bfloat16)
    low = (four - high.astype(np.float64)).astype(jnp.bfloat16)
    return np.stack([high, low, high.T, low.T])


def two_parts(value):
    high = value.astype(BF16)
    return high, (value - high.astype(F32)).astype(BF16)


def rows_by_rows(left, right):
    return lax.dot_general(left, right, (((1,), (1,)), ((), ())), preferred_element_type=F32)


def rows_by_cols(left, right):
    return lax.dot_general(left, right, (((1,), (0,)), ((), ())), preferred_element_type=F32)


def product(dot, left, right):
    return dot(left[0], right[0]) + dot(left[0], right[1]) + dot(left[1], right[0])


def one_hot_rows(place, lines, dtype):
    line = lax.broadcasted_iota(jnp.int32, (lines, place.shape[1]), 0)
    return jnp.where(line == place, 1.0, 0.0).astype(dtype)


def split_place(flat):
    lane = lax.broadcasted_iota(jnp.int32, flat.shape, 1)
    return (flat >> 6) + ((lane >> 5) << 6), flat & 63


def spread(values, column):
    line = lax.broadcasted_iota(jnp.int32, (GROUP, values.shape[1]), 0)
    return two_parts(jnp.where(line == column, values, 0.0))


def extract_kernel(momentum, grad, positions, table, out, m_in, g_in, p_in, basis, places, sems):
    copies = []
    for half in range(2):
        columns = pl.ds(512 * half, 512)
        copies.append((momentum.at[:, columns], m_in.at[half]))
        copies.append((grad.at[:, columns], g_in.at[half]))
        if half == 0:
            copies.append((table.at[pl.ds(0, 2)], basis))
            copies.append((positions, p_in))
    copies = [pltpu.make_async_copy(*pair, sems.at[n]) for n, pair in enumerate(copies)]
    for copy in copies:
        copy.start()
    for half in range(2):
        for copy in copies[4:] if half else copies[:4]:
            copy.wait()
        if half == 0:
            for x in range(4):
                places[:, 32 * x : 32 * x + 32] = p_in[x]
        straight = (basis[0], basis[1])
        moved = beta_decay * m_in[half] + g_in[half].astype(F32)
        moved = [two_parts(moved[:, 256 * g : 256 * g + 256]) for g in range(2)]
        rows = [two_parts(product(rows_by_rows, straight, value)) for value in moved]
        coeff = [two_parts(product(rows_by_rows, value, straight)) for value in rows]
        for g in range(2):
            lines = []
            for q in range(4):
                at = 8 * half + 4 * g + q
                flat = places[at : at + 1, :]
                row, column = split_place(flat)
                block = jnp.concatenate([part[GROUP * q : GROUP * (q + 1)] for part in coeff[g]], axis=0)
                found = rows_by_cols(block, one_hot_rows(row, 4 * GROUP, BF16))
                found = found[:GROUP] + found[GROUP:]
                line = lax.broadcasted_iota(jnp.int32, found.shape, 0)
                lines.append(jnp.sum(jnp.where(line == column, found, 0.0), axis=0, keepdims=True))
                lines.append(flat.astype(F32))
            tile = jnp.concatenate(lines, axis=0)
            for z in range(4):
                out[4 * z + 2 * half + g] = tile


def extract(momentum, grad, positions, table):
    return pl.pallas_call(
        extract_kernel,
        in_specs=[HBM] * 4,
        out_specs=VMEM,
        out_shape=jax.ShapeDtypeStruct((16, 8, 128), F32),
        scratch_shapes=[
            pltpu.VMEM((2, 256, 512), F32),
            pltpu.VMEM((2, 256, 512), BF16),
            pltpu.VMEM((4, 16, 32), jnp.int32),
            pltpu.VMEM((2, 256, 256), BF16),
            pltpu.VMEM((16, 128), jnp.int32),
            pltpu.SemaphoreType.DMA((6,)),
        ],
        cost_estimate=pl.CostEstimate(flops=10**9, bytes_accessed=2 * 2**20, transcendentals=0),
        compiler_params=limit(59),
        name="extract",
    )(momentum, grad, positions, table)


def kept_kernel(momentum, grad, sent, basis, far, out, token):
    straight, turned = (basis[0], basis[1]), (basis[2], basis[3])
    grids = []
    for g in range(2):
        tile, blocks = sent[g], []
        for q in range(4):
            row, column = split_place(tile[2 * q + 1 : 2 * q + 2].astype(jnp.int32))
            high, low = spread(tile[2 * q : 2 * q + 1], column)
            hot = one_hot_rows(row, 4 * GROUP, BF16)
            blocks.append(rows_by_rows(high, hot) + rows_by_rows(low, hot))
        grids.append(two_parts(jnp.concatenate(blocks, axis=0)))
    half = [two_parts(product(rows_by_rows, turned, grid)) for grid in grids]
    dense = [product(rows_by_cols, value, straight) for value in half]
    moved = beta_decay * momentum[...] + grad[...].astype(F32)
    for g in range(2):
        columns = slice(256 * g, 256 * g + 256)
        out[:, columns] = moved[:, columns] - dense[g]
    token[...] = jnp.zeros_like(token)


def kept(momentum, grad, sent, table, far):
    block = pl.BlockSpec((256, 512), lambda g: (0, g))
    whole = lambda *shape: pl.BlockSpec(shape, lambda g: (0,) * len(shape))
    return pl.pallas_call(
        kept_kernel,
        grid=(2,),
        in_specs=[block, block, pl.BlockSpec((2, 8, 128), lambda g: (g, 0, 0)), whole(4, 256, 256), ANY],
        out_specs=[block, whole(8, 128)],
        out_shape=[jax.ShapeDtypeStruct((256, 1024), F32), jax.ShapeDtypeStruct((8, 128), F32)],
        cost_estimate=pl.CostEstimate(flops=2 * 10**9, bytes_accessed=3 * 2**20, transcendentals=0),
        compiler_params=limit(12),
        name="kept",
    )(momentum, grad, sent, table, far)


def decode_kernel(*refs):
    entries, (weight, basis, fresh, smooth_out) = refs[:2], refs[2:]
    core = lax.axis_index("c")
    place = pl.multiple_of((lax.axis_index("y") * 2 + core) * 128, 128)
    tiles = []
    for ref in entries:
        for source in range(16):
            tile = ref[source]
            tiles.append(jnp.where(core == 0, tile[:4], tile[4:]))
    totals = [jnp.zeros((2 * GROUP, 4 * GROUP), F32)] * 2
    for pair in range(0, len(tiles), 2):
        for j in range(2):
            lefts, hots = [], []
            for tile in tiles[pair : pair + 2]:
                row, line = split_place(tile[2 * j + 1 : 2 * j + 2].astype(jnp.int32))
                lefts.append(jnp.concatenate(spread(tile[2 * j : 2 * j + 1], line), axis=0))
                hots.append(one_hot_rows(row, 4 * GROUP, BF16))
            found = rows_by_rows(jnp.concatenate(lefts, axis=1), jnp.concatenate(hots, axis=1))
            totals[j] = totals[j] + found
    blocks = [total[:GROUP] + total[GROUP:] for total in totals]
    grid = two_parts(jnp.concatenate(blocks, axis=0))
    half = product(rows_by_rows, (basis[2], basis[3]), grid)
    dense = product(rows_by_cols, two_parts(half), (basis[0, :128, :128], basis[1, :128, :128]))
    smooth = jnp.tanh(dense)
    smooth_out[0] = smooth.astype(BF16)
    fresh[0] = (weight[:, pl.ds(place, 128)].astype(F32) - step_rate * smooth).astype(BF16)


def decode(entries, weight, table):
    return pl.pallas_call(
        decode_kernel,
        in_specs=[VMEM] * 4,
        out_specs=[VMEM] * 2,
        out_shape=[jax.ShapeDtypeStruct((1, 256, 128), BF16)] * 2,
        cost_estimate=pl.CostEstimate(flops=10**9, bytes_accessed=2**20, transcendentals=32768),
        compiler_params=limit(12),
        name="decode",
    )(*entries, weight, table)


def near_kernel(a, b, c, d, out):
    for k, ref in enumerate((a, b, c, d)):
        out[k] = ref[0]


def join_near(arrays):
    return pl.pallas_call(
        near_kernel,
        in_specs=[VMEM] * 4,
        out_specs=VMEM,
        out_shape=jax.ShapeDtypeStruct((4, 256, 128), BF16),
        compiler_params=limit(4),
        name="join_near",
    )(*arrays)


def far_kernel(a, b, c, d, out):
    for k, ref in enumerate((a, b, c, d)):
        out[k] = ref[0]
        out[4 + k] = ref[1]


def join_far(arrays):
    return pl.pallas_call(
        far_kernel,
        in_specs=[VMEM] * 4,
        out_specs=VMEM,
        out_shape=jax.ShapeDtypeStruct((8, 256, 128), BF16),
        compiler_params=limit(4),
        name="join_far",
    )(*arrays)


def piece_copies(groups, pieces, out, sems):
    core, x, y, zl = (lax.axis_index(name) for name in ("c", "x", "y", "zl"))
    copies = []
    at = 0
    for k2, zs, others in groups:
        for other in others:
            at_core = jnp.bitwise_xor(core, other)
            for i, dz in enumerate(zs):
                for k1 in range(4):
                    first, second = (0, *RING)[k1], (0, *RING)[k2]
                    dx = jnp.where(at_core == 0, first, second)
                    dy = jnp.where(at_core == 0, second, first)
                    shard = jnp.bitwise_xor(x, dx) * 2 + jnp.bitwise_xor(zl, dz)
                    tile = shard * 8 + jnp.bitwise_xor(y, dy) * 2 + at_core
                    columns = pl.ds(pl.multiple_of(tile * 128, 128), 128)
                    copies.append(
                        pltpu.make_async_copy(
                            pieces[at].at[4 * i + k1], out.at[:, columns], sems.at[len(copies)]
                        )
                    )
            at += 1
    return copies


def count_copies(groups):
    return sum(4 * len(zs) * len(others) for _, zs, others in groups)


NEW_WEIGHT = jax.ShapeDtypeStruct((256, 8192), BF16)
LAID = jax.ShapeDtypeStruct((256, 1024), BF16)


def lay_kernel(groups, *refs):
    firsts, pieces, (laid, out, sems) = refs[:4], refs[5:-3], refs[-3:]
    copies = piece_copies(groups, pieces, out, sems)
    for copy in copies:
        copy.start()
    core, y = lax.axis_index("c"), lax.axis_index("y")
    for k in range(4):
        for other in range(2):
            tile = jnp.bitwise_xor(y, (0, *RING)[k]) * 2 + jnp.bitwise_xor(core, other)
            laid[:, pl.ds(pl.multiple_of(tile * 128, 128), 128)] = firsts[k][2 + other]
    for copy in copies:
        copy.wait()


def lay(firsts, token, groups, pieces):
    return pl.pallas_call(
        functools.partial(lay_kernel, groups),
        in_specs=[VMEM] * 4 + [ANY] * (1 + len(pieces)),
        out_specs=[VMEM, ANY],
        out_shape=[LAID, NEW_WEIGHT],
        scratch_shapes=[pltpu.SemaphoreType.DMA((count_copies(groups),))],
        compiler_params=limit(4),
        name="lay",
    )(*firsts, token, *pieces)


def choose_kernel(groups, mine, theirs, *refs):
    pieces, (direction, out, sems, sem) = refs[:-5], refs[-4:]
    copies = piece_copies(groups, pieces, out, sems)
    for copy in copies:
        copy.start()
    for core, source in enumerate((theirs, mine)):

        @pl.when(lax.axis_index("c") == core)
        def _():
            copy = pltpu.make_async_copy(source, direction, sem)
            copy.start()
            copy.wait()

    for copy in copies:
        copy.wait()


def choose(mine, theirs, groups, pieces, done):
    return pl.pallas_call(
        functools.partial(choose_kernel, groups),
        in_specs=[ANY] * (3 + len(pieces)),
        out_specs=[ANY] * 2,
        out_shape=[LAID, NEW_WEIGHT],
        scratch_shapes=[pltpu.SemaphoreType.DMA((count_copies(groups),)), pltpu.SemaphoreType.DMA],
        input_output_aliases={2 + len(pieces): 1},
        compiler_params=limit(1),
        name="choose",
    )(mine, theirs, *pieces, done)


def finish_kernel(groups, *refs):
    pieces, (out, sems) = refs[:-3], refs[-2:]
    copies = piece_copies(groups, pieces, out, sems)
    for copy in copies:
        copy.start()
    for copy in copies:
        copy.wait()


def finish(groups, pieces, done):
    return pl.pallas_call(
        functools.partial(finish_kernel, groups),
        in_specs=[ANY] * (1 + len(pieces)),
        out_specs=ANY,
        out_shape=NEW_WEIGHT,
        scratch_shapes=[pltpu.SemaphoreType.DMA((count_copies(groups),))],
        input_output_aliases={len(pieces): 0},
        compiler_params=limit(1),
        name="finish",
    )(*pieces, done)


def swapped(array, axis, size, k):
    return lax.ppermute(array, axis, [(i, i ^ k) for i in range(size)])


def crossed(array, first, k):
    perm = []
    for i in range(32):
        y, c, x = i >> 3, (i >> 2) & 1, i & 3
        to = (y, c, x ^ k) if c == first else (y ^ k, c, x)
        perm.append((i, (to[0] << 3) | (to[1] << 2) | to[2]))
    return lax.ppermute(array, ("y", "c", "x"), perm)


def other_core(array):
    return swapped(array, "c", 2, 1)


def per_device(weight, momentum, grad, positions):
    table = jnp.asarray(basis_parts())
    sent = extract(momentum[0], grad[0], positions[0], table)
    arrived = lax.all_to_all(sent, ("zh", "y"), 0, 0, tiled=True)
    fresh, smooth = decode([arrived, other_core(arrived)], other_core(weight), other_core(table))
    near = join_near([fresh, swapped(fresh, "zl", 2, 1), smooth, other_core(smooth)])
    firsts = [near] + [crossed(near, 0, k) for k in RING]
    far = join_far(firsts)
    kept_state, token = kept(momentum[0], grad[0], sent, table, far)
    one, two, three = (crossed(far, 1, k) for k in RING)
    both = lambda array: [array, other_core(array)]
    laid, new_weight = lay(firsts, token, [(0, (0, 1), (0,))], [far])
    direction, new_weight = choose(
        laid,
        other_core(laid),
        [(0, (0, 1), (1,)), (1, (0, 1), (0, 1))],
        [other_core(far)] + both(one),
        new_weight,
    )
    new_weight = finish([(2, (0, 1), (0, 1)), (3, (0, 1), (0, 1))], both(two) + both(three), new_weight)
    return (kept_state[None], direction, new_weight)


def solution(mesh):
    split = Mesh(mesh.devices.reshape(4, 4, 2, 4, 2), ("zh", "y", "c", "x", "zl"))
    in_specs = (
        P(None, SHARD),
        P(REPLICA, None, SHARD),
        P(REPLICA, None, SHARD),
        P(REPLICA, None, SHARD, None),
    )
    out_specs = (P(REPLICA, None, SHARD), P(None, SHARD), P())
    return jax.shard_map(
        per_device, mesh=split, in_specs=in_specs, out_specs=out_specs, check_vma=False
    )
```

```python
import functools
import math

import jax
import jax.numpy as jnp
import numpy as np
from jax import lax
from jax.experimental import pallas as pl
from jax.experimental.pallas import tpu as pltpu
from jax.sharding import Mesh
from jax.sharding import PartitionSpec as P

GROUP = 64
REPLICA = ("zh", "y", "c")
SHARD = ("x", "zl")
beta_decay = 0.9
step_rate = 0.02
F32, BF16 = jnp.float32, jnp.bfloat16
VMEM = pl.BlockSpec(memory_space=pltpu.VMEM)
RING = (1, 3, 2)
ANY = pl.BlockSpec(memory_space=pl.ANY)
HBM = pl.BlockSpec(memory_space=pltpu.HBM)


def limit(mib):
    return pltpu.CompilerParams(vmem_limit_bytes=int(mib * 2**20))


def basis_parts():
    freq, cells = np.arange(GROUP)[:, None], np.arange(GROUP)[None, :]
    scales = np.where(freq == 0, math.sqrt(1.0 / GROUP), math.sqrt(2.0 / GROUP))
    table = scales * np.cos(math.pi * (2.0 * cells + 1.0) * freq / (2.0 * GROUP))
    four = np.kron(np.eye(4), table)
    high = four.astype(jnp.bfloat16)
    low = (four - high.astype(np.float64)).astype(jnp.bfloat16)
    return np.stack([high, low, high.T, low.T])


def two_parts(value):
    high = value.astype(BF16)
    return high, (value - high.astype(F32)).astype(BF16)


def rows_by_rows(left, right):
    return lax.dot_general(left, right, (((1,), (1,)), ((), ())), preferred_element_type=F32)


def rows_by_cols(left, right):
    return lax.dot_general(left, right, (((1,), (0,)), ((), ())), preferred_element_type=F32)


def product(dot, left, right):
    lines = left[0].shape[0]
    both = dot(jnp.concatenate(left, axis=0), right[0])
    return both[:lines] + both[lines:] + dot(left[0], right[1])


def one_hot_rows(place, lines, dtype):
    line = lax.broadcasted_iota(jnp.int32, (lines, place.shape[1]), 0)
    return jnp.where(line == place, 1.0, 0.0).astype(dtype)


def split_place(flat):
    lane = lax.broadcasted_iota(jnp.int32, flat.shape, 1)
    return (flat >> 6) + ((lane >> 5) << 6), flat & 63


def spread(values, column):
    line = lax.broadcasted_iota(jnp.int32, (GROUP, values.shape[1]), 0)
    return two_parts(jnp.where(line == column, values, 0.0))


def extract_kernel(momentum, grad, positions, table, out, m_in, g_in, p_in, basis, places, sems):
    copies = []
    for half in range(2):
        columns = pl.ds(512 * half, 512)
        copies.append((momentum.at[:, columns], m_in.at[half]))
        copies.append((grad.at[:, columns], g_in.at[half]))
        if half == 0:
            copies.append((table, basis))
            copies.append((positions, p_in))
    copies = [pltpu.make_async_copy(*pair, sems.at[n]) for n, pair in enumerate(copies)]
    for copy in copies:
        copy.start()
    for half in range(2):
        for copy in copies[4:] if half else copies[:4]:
            copy.wait()
        if half == 0:
            for x in range(4):
                places[:, 32 * x : 32 * x + 32] = p_in[x]
        straight, turned = (basis[0], basis[1]), (basis[2], basis[3])
        moved = beta_decay * m_in[half] + g_in[half].astype(F32)
        moved = [two_parts(moved[:, 256 * g : 256 * g + 256]) for g in range(2)]
        rows = [two_parts(product(rows_by_rows, straight, value)) for value in moved]
        coeff = [two_parts(product(rows_by_cols, value, turned)) for value in rows]
        for g in range(2):
            lines = []
            for q in range(4):
                at = 8 * half + 4 * g + q
                flat = places[at : at + 1, :]
                row, column = split_place(flat)
                block = jnp.concatenate([part[GROUP * q : GROUP * (q + 1)] for part in coeff[g]], axis=0)
                found = rows_by_cols(block, one_hot_rows(row, 4 * GROUP, BF16))
                found = found[:GROUP] + found[GROUP:]
                line = lax.broadcasted_iota(jnp.int32, found.shape, 0)
                lines.append(jnp.sum(jnp.where(line == column, found, 0.0), axis=0, keepdims=True))
                lines.append(flat.astype(F32))
            tile = jnp.concatenate(lines, axis=0)
            for z in range(4):
                out[4 * z + 2 * half + g] = tile


def extract(momentum, grad, positions, table):
    return pl.pallas_call(
        extract_kernel,
        in_specs=[HBM] * 4,
        out_specs=VMEM,
        out_shape=jax.ShapeDtypeStruct((16, 8, 128), F32),
        scratch_shapes=[
            pltpu.VMEM((2, 256, 512), F32),
            pltpu.VMEM((2, 256, 512), BF16),
            pltpu.VMEM((4, 16, 32), jnp.int32),
            pltpu.VMEM((4, 256, 256), BF16),
            pltpu.VMEM((16, 128), jnp.int32),
            pltpu.SemaphoreType.DMA((6,)),
        ],
        cost_estimate=pl.CostEstimate(flops=10**9, bytes_accessed=2 * 2**20, transcendentals=0),
        compiler_params=limit(59),
        name="extract",
    )(momentum, grad, positions, table)


def kept_kernel(momentum, grad, sent, basis, far, out, token):
    straight, turned = (basis[0], basis[1]), (basis[2], basis[3])
    grids = []
    for g in range(2):
        tile, blocks = sent[g], []
        for q in range(4):
            row, column = split_place(tile[2 * q + 1 : 2 * q + 2].astype(jnp.int32))
            high, low = spread(tile[2 * q : 2 * q + 1], column)
            hot = one_hot_rows(row, 4 * GROUP, BF16)
            blocks.append(rows_by_rows(high, hot) + rows_by_rows(low, hot))
        grids.append(two_parts(jnp.concatenate(blocks, axis=0)))
    half = [two_parts(product(rows_by_rows, turned, grid)) for grid in grids]
    dense = [product(rows_by_cols, value, straight) for value in half]
    moved = beta_decay * momentum[...] + grad[...].astype(F32)
    for g in range(2):
        columns = slice(256 * g, 256 * g + 256)
        out[:, columns] = moved[:, columns] - dense[g]
    token[...] = jnp.zeros_like(token)


def kept(momentum, grad, sent, table, far):
    block = pl.BlockSpec((256, 512), lambda g: (0, g))
    whole = lambda *shape: pl.BlockSpec(shape, lambda g: (0,) * len(shape))
    return pl.pallas_call(
        kept_kernel,
        grid=(2,),
        in_specs=[block, block, pl.BlockSpec((2, 8, 128), lambda g: (g, 0, 0)), whole(4, 256, 256), ANY],
        out_specs=[block, whole(8, 128)],
        out_shape=[jax.ShapeDtypeStruct((256, 1024), F32), jax.ShapeDtypeStruct((8, 128), F32)],
        cost_estimate=pl.CostEstimate(flops=2 * 10**9, bytes_accessed=3 * 2**20, transcendentals=0),
        compiler_params=limit(12),
        name="kept",
    )(momentum, grad, sent, table, far)


def gather_entries(arrived, totals):
    core = lax.axis_index("c")
    tiles = []
    for source in range(16):
        tile = arrived[source]
        tiles.append(jnp.where(core == 0, tile[:4], tile[4:]))
    for pair in range(0, len(tiles), 2):
        for j in range(2):
            lefts, hots = [], []
            for tile in tiles[pair : pair + 2]:
                row, line = split_place(tile[2 * j + 1 : 2 * j + 2].astype(jnp.int32))
                lefts.append(jnp.concatenate(spread(tile[2 * j : 2 * j + 1], line), axis=0))
                hots.append(one_hot_rows(row, 4 * GROUP, BF16))
            found = rows_by_rows(jnp.concatenate(lefts, axis=1), jnp.concatenate(hots, axis=1))
            totals[j] = found if totals[j] is None else totals[j] + found
    return [total[:GROUP] + total[GROUP:] for total in totals]


def begin_kernel(arrived, out):
    for j, total in enumerate(gather_entries(arrived, [None, None])):
        out[GROUP * j : GROUP * (j + 1)] = total


def begin(arrived):
    return pl.pallas_call(
        begin_kernel,
        in_specs=[VMEM],
        out_specs=VMEM,
        out_shape=jax.ShapeDtypeStruct((2 * GROUP, 4 * GROUP), F32),
        cost_estimate=pl.CostEstimate(flops=10**9, bytes_accessed=2**20, transcendentals=0),
        compiler_params=limit(8),
        name="begin",
    )(arrived)


def decode_kernel(begun, arrived, weight, basis, fresh, smooth_out):
    place = pl.multiple_of((lax.axis_index("y") * 2 + lax.axis_index("c")) * 128, 128)
    blocks = gather_entries(arrived, [None, None])
    grid = two_parts(begun[...] + jnp.concatenate(blocks, axis=0))
    half = product(rows_by_rows, (basis[2], basis[3]), grid)
    dense = product(rows_by_cols, two_parts(half), (basis[0, :128, :128], basis[1, :128, :128]))
    smooth = jnp.tanh(dense)
    smooth_out[0] = smooth.astype(BF16)
    fresh[0] = (weight[:, pl.ds(place, 128)].astype(F32) - step_rate * smooth).astype(BF16)


def decode(begun, arrived, weight, table):
    return pl.pallas_call(
        decode_kernel,
        in_specs=[VMEM] * 4,
        out_specs=[VMEM] * 2,
        out_shape=[jax.ShapeDtypeStruct((1, 256, 128), BF16)] * 2,
        cost_estimate=pl.CostEstimate(flops=10**9, bytes_accessed=2**20, transcendentals=32768),
        compiler_params=limit(8),
        name="decode",
    )(begun, arrived, weight, table)


def near_kernel(a, b, c, d, out):
    for k, ref in enumerate((a, b, c, d)):
        out[k] = ref[0]


def join_near(arrays):
    return pl.pallas_call(
        near_kernel,
        in_specs=[VMEM] * 4,
        out_specs=VMEM,
        out_shape=jax.ShapeDtypeStruct((4, 256, 128), BF16),
        compiler_params=limit(4),
        name="join_near",
    )(*arrays)


def far_kernel(a, b, c, d, out):
    for k, ref in enumerate((a, b, c, d)):
        out[k] = ref[0]
        out[4 + k] = ref[1]


def join_far(arrays):
    return pl.pallas_call(
        far_kernel,
        in_specs=[VMEM] * 4,
        out_specs=VMEM,
        out_shape=jax.ShapeDtypeStruct((8, 256, 128), BF16),
        compiler_params=limit(4),
        name="join_far",
    )(*arrays)


def piece_copies(groups, pieces, out, sems):
    core, x, y, zl = (lax.axis_index(name) for name in ("c", "x", "y", "zl"))
    copies = []
    at = 0
    for k2, zs, others in groups:
        for other in others:
            at_core = jnp.bitwise_xor(core, other)
            for i, dz in enumerate(zs):
                for k1 in range(4):
                    first, second = (0, *RING)[k1], (0, *RING)[k2]
                    dx = jnp.where(at_core == 0, first, second)
                    dy = jnp.where(at_core == 0, second, first)
                    shard = jnp.bitwise_xor(x, dx) * 2 + jnp.bitwise_xor(zl, dz)
                    tile = shard * 8 + jnp.bitwise_xor(y, dy) * 2 + at_core
                    columns = pl.ds(pl.multiple_of(tile * 128, 128), 128)
                    copies.append(
                        pltpu.make_async_copy(
                            pieces[at].at[4 * i + k1], out.at[:, columns], sems.at[len(copies)]
                        )
                    )
            at += 1
    return copies


def count_copies(groups):
    return sum(4 * len(zs) * len(others) for _, zs, others in groups)


NEW_WEIGHT = jax.ShapeDtypeStruct((256, 8192), BF16)
LAID = jax.ShapeDtypeStruct((256, 1024), BF16)


def lay_kernel(groups, *refs):
    firsts, pieces, (laid, out, sems) = refs[:4], refs[5:-3], refs[-3:]
    copies = piece_copies(groups, pieces, out, sems)
    for copy in copies:
        copy.start()
    core, y = lax.axis_index("c"), lax.axis_index("y")
    for k in range(4):
        for other in range(2):
            tile = jnp.bitwise_xor(y, (0, *RING)[k]) * 2 + jnp.bitwise_xor(core, other)
            laid[:, pl.ds(pl.multiple_of(tile * 128, 128), 128)] = firsts[k][2 + other]
    for copy in copies:
        copy.wait()


def lay(firsts, token, groups, pieces):
    return pl.pallas_call(
        functools.partial(lay_kernel, groups),
        in_specs=[VMEM] * 4 + [ANY] * (1 + len(pieces)),
        out_specs=[VMEM, ANY],
        out_shape=[LAID, NEW_WEIGHT],
        scratch_shapes=[pltpu.SemaphoreType.DMA((count_copies(groups),))],
        compiler_params=limit(4),
        name="lay",
    )(*firsts, token, *pieces)


def choose_kernel(groups, mine, theirs, *refs):
    pieces, (direction, out, sems, sem) = refs[:-5], refs[-4:]
    copies = piece_copies(groups, pieces, out, sems)
    for copy in copies:
        copy.start()
    for core, source in enumerate((theirs, mine)):

        @pl.when(lax.axis_index("c") == core)
        def _():
            copy = pltpu.make_async_copy(source, direction, sem)
            copy.start()
            copy.wait()

    for copy in copies:
        copy.wait()


def choose(mine, theirs, groups, pieces, done):
    return pl.pallas_call(
        functools.partial(choose_kernel, groups),
        in_specs=[ANY] * (3 + len(pieces)),
        out_specs=[ANY] * 2,
        out_shape=[LAID, NEW_WEIGHT],
        scratch_shapes=[pltpu.SemaphoreType.DMA((count_copies(groups),)), pltpu.SemaphoreType.DMA],
        input_output_aliases={2 + len(pieces): 1},
        compiler_params=limit(1),
        name="choose",
    )(mine, theirs, *pieces, done)


def finish_kernel(groups, *refs):
    pieces, (out, sems) = refs[:-3], refs[-2:]
    copies = piece_copies(groups, pieces, out, sems)
    for copy in copies:
        copy.start()
    for copy in copies:
        copy.wait()


def finish(groups, pieces, done):
    return pl.pallas_call(
        functools.partial(finish_kernel, groups),
        in_specs=[ANY] * (1 + len(pieces)),
        out_specs=ANY,
        out_shape=NEW_WEIGHT,
        scratch_shapes=[pltpu.SemaphoreType.DMA((count_copies(groups),))],
        input_output_aliases={len(pieces): 0},
        compiler_params=limit(1),
        name="finish",
    )(*pieces, done)


def swapped(array, axis, size, k):
    return lax.ppermute(array, axis, [(i, i ^ k) for i in range(size)])


def crossed(array, first, k):
    perm = []
    for i in range(32):
        y, c, x = i >> 3, (i >> 2) & 1, i & 3
        to = (y, c, x ^ k) if c == first else (y ^ k, c, x)
        perm.append((i, (to[0] << 3) | (to[1] << 2) | to[2]))
    return lax.ppermute(array, ("y", "c", "x"), perm)


def other_core(array):
    return swapped(array, "c", 2, 1)


def per_device(weight, momentum, grad, positions):
    table = jnp.asarray(basis_parts())
    sent = extract(momentum[0], grad[0], positions[0], table)
    arrived = lax.all_to_all(sent, ("zh", "y"), 0, 0, tiled=True)
    fresh, smooth = decode(begin(arrived), other_core(arrived), other_core(weight), other_core(table))
    near = join_near([fresh, swapped(fresh, "zl", 2, 1), smooth, other_core(smooth)])
    firsts = [near] + [crossed(near, 0, k) for k in RING]
    far = join_far(firsts)
    kept_state, token = kept(momentum[0], grad[0], sent, table, far)
    one, two, three = (crossed(far, 1, k) for k in RING)
    laid, new_weight = lay(firsts, token, [(0, (0, 1), (0,)), (1, (0, 1), (0,))], [far, one])
    direction, new_weight = choose(
        laid,
        other_core(laid),
        [(0, (0, 1), (1,)), (1, (0, 1), (1,)), (2, (0, 1), (0,)), (3, (0, 1), (0,))],
        [other_core(far), other_core(one), two, three],
        new_weight,
    )
    new_weight = finish(
        [(2, (0, 1), (1,)), (3, (0, 1), (1,))], [other_core(two), other_core(three)], new_weight
    )
    return (kept_state[None], direction, new_weight)


def solution(mesh):
    split = Mesh(mesh.devices.reshape(4, 4, 2, 4, 2), ("zh", "y", "c", "x", "zl"))
    in_specs = (
        P(None, SHARD),
        P(REPLICA, None, SHARD),
        P(REPLICA, None, SHARD),
        P(REPLICA, None, SHARD, None),
    )
    out_specs = (P(REPLICA, None, SHARD), P(None, SHARD), P())
    return jax.shard_map(
        per_device, mesh=split, in_specs=in_specs, out_specs=out_specs, check_vma=False
    )
```

```python
import functools
import math

import jax
import jax.numpy as jnp
import numpy as np
from jax import lax
from jax.experimental import pallas as pl
from jax.experimental.pallas import tpu as pltpu
from jax.sharding import Mesh
from jax.sharding import PartitionSpec as P

GROUP = 64
REPLICA = ("zh", "y", "c")
SHARD = ("x", "zl")
beta_decay = 0.9
step_rate = 0.02
F32, BF16 = jnp.float32, jnp.bfloat16
VMEM = pl.BlockSpec(memory_space=pltpu.VMEM)
RING = (1, 3, 2)
ANY = pl.BlockSpec(memory_space=pl.ANY)
HBM = pl.BlockSpec(memory_space=pltpu.HBM)


def limit(mib):
    return pltpu.CompilerParams(vmem_limit_bytes=int(mib * 2**20))


def basis_parts():
    freq, cells = np.arange(GROUP)[:, None], np.arange(GROUP)[None, :]
    scales = np.where(freq == 0, math.sqrt(1.0 / GROUP), math.sqrt(2.0 / GROUP))
    table = scales * np.cos(math.pi * (2.0 * cells + 1.0) * freq / (2.0 * GROUP))
    four = np.kron(np.eye(4), table)
    high = four.astype(jnp.bfloat16)
    low = (four - high.astype(np.float64)).astype(jnp.bfloat16)
    return np.stack([high, low, high.T, low.T])


def two_parts(value):
    high = value.astype(BF16)
    return high, (value - high.astype(F32)).astype(BF16)


def rows_by_rows(left, right):
    return lax.dot_general(left, right, (((1,), (1,)), ((), ())), preferred_element_type=F32)


def rows_by_cols(left, right):
    return lax.dot_general(left, right, (((1,), (0,)), ((), ())), preferred_element_type=F32)


def product(dot, left, right):
    lines = left[0].shape[0]
    both = dot(jnp.concatenate(left, axis=0), right[0])
    return both[:lines] + both[lines:] + dot(left[0], right[1])


def one_hot_rows(place, lines, dtype):
    line = lax.broadcasted_iota(jnp.int32, (lines, place.shape[1]), 0)
    return jnp.where(line == place, 1.0, 0.0).astype(dtype)


def split_place(flat):
    lane = lax.broadcasted_iota(jnp.int32, flat.shape, 1)
    return (flat >> 6) + ((lane >> 5) << 6), flat & 63


def spread(values, column):
    line = lax.broadcasted_iota(jnp.int32, (GROUP, values.shape[1]), 0)
    return two_parts(jnp.where(line == column, values, 0.0))


def extract_kernel(momentum, grad, positions, table, out, m_in, g_in, p_in, basis, places, sems):
    copies = []
    for half in range(2):
        columns = pl.ds(512 * half, 512)
        copies.append((momentum.at[:, columns], m_in.at[half]))
        copies.append((grad.at[:, columns], g_in.at[half]))
        if half == 0:
            copies.append((table, basis))
            copies.append((positions, p_in))
    copies = [pltpu.make_async_copy(*pair, sems.at[n]) for n, pair in enumerate(copies)]
    for copy in copies:
        copy.start()
    for half in range(2):
        for copy in copies[4:] if half else copies[:4]:
            copy.wait()
        if half == 0:
            for x in range(4):
                places[:, 32 * x : 32 * x + 32] = p_in[x]
        straight, turned = (basis[0], basis[1]), (basis[2], basis[3])
        moved = beta_decay * m_in[half] + g_in[half].astype(F32)
        moved = [two_parts(moved[:, 256 * g : 256 * g + 256]) for g in range(2)]
        rows = [two_parts(product(rows_by_rows, straight, value)) for value in moved]
        coeff = [two_parts(product(rows_by_cols, value, turned)) for value in rows]
        for g in range(2):
            lines = []
            for q in range(4):
                at = 8 * half + 4 * g + q
                flat = places[at : at + 1, :]
                row, column = split_place(flat)
                block = jnp.concatenate([part[GROUP * q : GROUP * (q + 1)] for part in coeff[g]], axis=0)
                found = rows_by_cols(block, one_hot_rows(row, 4 * GROUP, BF16))
                found = found[:GROUP] + found[GROUP:]
                line = lax.broadcasted_iota(jnp.int32, found.shape, 0)
                lines.append(jnp.sum(jnp.where(line == column, found, 0.0), axis=0, keepdims=True))
                lines.append(flat.astype(F32))
            tile = jnp.concatenate(lines, axis=0)
            for z in range(4):
                out[4 * z + 2 * half + g] = tile


def extract(momentum, grad, positions, table):
    return pl.pallas_call(
        extract_kernel,
        in_specs=[HBM] * 4,
        out_specs=VMEM,
        out_shape=jax.ShapeDtypeStruct((16, 8, 128), F32),
        scratch_shapes=[
            pltpu.VMEM((2, 256, 512), F32),
            pltpu.VMEM((2, 256, 512), BF16),
            pltpu.VMEM((4, 16, 32), jnp.int32),
            pltpu.VMEM((4, 256, 256), BF16),
            pltpu.VMEM((16, 128), jnp.int32),
            pltpu.SemaphoreType.DMA((6,)),
        ],
        cost_estimate=pl.CostEstimate(flops=10**9, bytes_accessed=2 * 2**20, transcendentals=0),
        compiler_params=limit(59),
        name="extract",
    )(momentum, grad, positions, table)


def kept_kernel(momentum, grad, sent, basis, far, out, token):
    straight, turned = (basis[0], basis[1]), (basis[2], basis[3])
    grids = []
    for g in range(2):
        tile, blocks = sent[g], []
        for q in range(4):
            row, column = split_place(tile[2 * q + 1 : 2 * q + 2].astype(jnp.int32))
            high, low = spread(tile[2 * q : 2 * q + 1], column)
            hot = one_hot_rows(row, 4 * GROUP, BF16)
            blocks.append(rows_by_rows(high, hot) + rows_by_rows(low, hot))
        grids.append(two_parts(jnp.concatenate(blocks, axis=0)))
    half = [two_parts(product(rows_by_rows, turned, grid)) for grid in grids]
    dense = [product(rows_by_cols, value, straight) for value in half]
    moved = beta_decay * momentum[...] + grad[...].astype(F32)
    for g in range(2):
        columns = slice(256 * g, 256 * g + 256)
        out[:, columns] = moved[:, columns] - dense[g]
    token[...] = jnp.zeros_like(token)


def kept(momentum, grad, sent, table, far):
    block = pl.BlockSpec((256, 512), lambda g: (0, g))
    whole = lambda *shape: pl.BlockSpec(shape, lambda g: (0,) * len(shape))
    return pl.pallas_call(
        kept_kernel,
        grid=(2,),
        in_specs=[block, block, pl.BlockSpec((2, 8, 128), lambda g: (g, 0, 0)), whole(4, 256, 256), ANY],
        out_specs=[block, whole(8, 128)],
        out_shape=[jax.ShapeDtypeStruct((256, 1024), F32), jax.ShapeDtypeStruct((8, 128), F32)],
        cost_estimate=pl.CostEstimate(flops=2 * 10**9, bytes_accessed=3 * 2**20, transcendentals=0),
        compiler_params=limit(12),
        name="kept",
    )(momentum, grad, sent, table, far)


def gather_entries(arrived, totals):
    core = lax.axis_index("c")
    tiles = []
    for source in range(16):
        tile = arrived[source]
        tiles.append(jnp.where(core == 0, tile[:4], tile[4:]))
    for pair in range(0, len(tiles), 2):
        for j in range(2):
            lefts, hots = [], []
            for tile in tiles[pair : pair + 2]:
                row, line = split_place(tile[2 * j + 1 : 2 * j + 2].astype(jnp.int32))
                lefts.append(jnp.concatenate(spread(tile[2 * j : 2 * j + 1], line), axis=0))
                hots.append(one_hot_rows(row, 4 * GROUP, BF16))
            found = rows_by_rows(jnp.concatenate(lefts, axis=1), jnp.concatenate(hots, axis=1))
            totals[j] = found if totals[j] is None else totals[j] + found
    return [total[:GROUP] + total[GROUP:] for total in totals]


def begin_kernel(arrived, out):
    for j, total in enumerate(gather_entries(arrived, [None, None])):
        out[GROUP * j : GROUP * (j + 1)] = total


def begin(arrived):
    return pl.pallas_call(
        begin_kernel,
        in_specs=[VMEM],
        out_specs=VMEM,
        out_shape=jax.ShapeDtypeStruct((2 * GROUP, 4 * GROUP), F32),
        cost_estimate=pl.CostEstimate(flops=10**9, bytes_accessed=2**20, transcendentals=0),
        compiler_params=limit(8),
        name="begin",
    )(arrived)


def decode_kernel(begun, arrived, weight, basis, fresh, smooth_out):
    place = pl.multiple_of((lax.axis_index("y") * 2 + lax.axis_index("c")) * 128, 128)
    blocks = gather_entries(arrived, [None, None])
    grid = two_parts(begun[...] + jnp.concatenate(blocks, axis=0))
    half = product(rows_by_rows, (basis[2], basis[3]), grid)
    dense = product(rows_by_cols, two_parts(half), (basis[0, :128, :128], basis[1, :128, :128]))
    smooth = jnp.tanh(dense)
    smooth_out[0] = smooth.astype(BF16)
    fresh[0] = (weight[:, pl.ds(place, 128)].astype(F32) - step_rate * smooth).astype(BF16)


def decode(begun, arrived, weight, table):
    return pl.pallas_call(
        decode_kernel,
        in_specs=[VMEM] * 4,
        out_specs=[VMEM] * 2,
        out_shape=[jax.ShapeDtypeStruct((1, 256, 128), BF16)] * 2,
        cost_estimate=pl.CostEstimate(flops=10**9, bytes_accessed=2**20, transcendentals=32768),
        compiler_params=limit(8),
        name="decode",
    )(begun, arrived, weight, table)


def near_kernel(a, b, c, out):
    for k, ref in enumerate((a, b, c)):
        out[k] = ref[0]


def join_near(arrays):
    return pl.pallas_call(
        near_kernel,
        in_specs=[VMEM] * 3,
        out_specs=VMEM,
        out_shape=jax.ShapeDtypeStruct((3, 256, 128), BF16),
        compiler_params=limit(4),
        name="join_near",
    )(*arrays)


def four_kernel(near, fresh_z, out):
    out[:3] = near[...]
    out[3] = fresh_z[0]


def join_four(near, fresh_z):
    return pl.pallas_call(
        four_kernel,
        in_specs=[VMEM] * 2,
        out_specs=VMEM,
        out_shape=jax.ShapeDtypeStruct((4, 256, 128), BF16),
        compiler_params=limit(4),
        name="join_four",
    )(near, fresh_z)


def far_kernel(a, b, c, across, a_z, b_z, c_z, out):
    for k, ref in enumerate((a, b, c, across, a_z, b_z, c_z)):
        out[k] = ref[0]
    out[7] = across[3]


def join_far(arrays):
    return pl.pallas_call(
        far_kernel,
        in_specs=[VMEM] * 7,
        out_specs=VMEM,
        out_shape=jax.ShapeDtypeStruct((8, 256, 128), BF16),
        compiler_params=limit(4),
        name="join_far",
    )(*arrays)


def piece_copies(groups, pieces, out, sems):
    core, x, y, zl = (lax.axis_index(name) for name in ("c", "x", "y", "zl"))
    copies = []
    at = 0
    for k2, zs, others in groups:
        for other in others:
            at_core = jnp.bitwise_xor(core, other)
            for i, dz in enumerate(zs):
                for k1 in range(4):
                    first, second = (0, *RING)[k1], (0, *RING)[k2]
                    dx = jnp.where(at_core == 0, first, second)
                    dy = jnp.where(at_core == 0, second, first)
                    shard = jnp.bitwise_xor(x, dx) * 2 + jnp.bitwise_xor(zl, dz)
                    tile = shard * 8 + jnp.bitwise_xor(y, dy) * 2 + at_core
                    columns = pl.ds(pl.multiple_of(tile * 128, 128), 128)
                    copies.append(
                        pltpu.make_async_copy(
                            pieces[at].at[4 * i + k1], out.at[:, columns], sems.at[len(copies)]
                        )
                    )
            at += 1
    return copies


def count_copies(groups):
    return sum(4 * len(zs) * len(others) for _, zs, others in groups)


NEW_WEIGHT = jax.ShapeDtypeStruct((256, 8192), BF16)
LAID = jax.ShapeDtypeStruct((256, 1024), BF16)


def lay_kernel(groups, *refs):
    firsts, pieces, (laid, out, sems) = refs[:4], refs[5:-3], refs[-3:]
    copies = piece_copies(groups, pieces, out, sems)
    for copy in copies:
        copy.start()
    core, y = lax.axis_index("c"), lax.axis_index("y")
    for k in range(4):
        for other in range(2):
            tile = jnp.bitwise_xor(y, (0, *RING)[k]) * 2 + jnp.bitwise_xor(core, other)
            laid[:, pl.ds(pl.multiple_of(tile * 128, 128), 128)] = firsts[k][1 + other]
    for copy in copies:
        copy.wait()


def lay(firsts, token, groups, pieces):
    return pl.pallas_call(
        functools.partial(lay_kernel, groups),
        in_specs=[VMEM] * 4 + [ANY] * (1 + len(pieces)),
        out_specs=[VMEM, ANY],
        out_shape=[LAID, NEW_WEIGHT],
        scratch_shapes=[pltpu.SemaphoreType.DMA((count_copies(groups),))],
        compiler_params=limit(4),
        name="lay",
    )(*firsts, token, *pieces)


def choose_kernel(groups, mine, theirs, *refs):
    pieces, (direction, out, sems, sem) = refs[:-5], refs[-4:]
    copies = piece_copies(groups, pieces, out, sems)
    for copy in copies:
        copy.start()
    for core, source in enumerate((theirs, mine)):

        @pl.when(lax.axis_index("c") == core)
        def _():
            copy = pltpu.make_async_copy(source, direction, sem)
            copy.start()
            copy.wait()

    for copy in copies:
        copy.wait()


def choose(mine, theirs, groups, pieces, done):
    return pl.pallas_call(
        functools.partial(choose_kernel, groups),
        in_specs=[ANY] * (3 + len(pieces)),
        out_specs=[ANY] * 2,
        out_shape=[LAID, NEW_WEIGHT],
        scratch_shapes=[pltpu.SemaphoreType.DMA((count_copies(groups),)), pltpu.SemaphoreType.DMA],
        input_output_aliases={2 + len(pieces): 1},
        compiler_params=limit(1),
        name="choose",
    )(mine, theirs, *pieces, done)


def finish_kernel(groups, *refs):
    pieces, (out, sems) = refs[:-3], refs[-2:]
    copies = piece_copies(groups, pieces, out, sems)
    for copy in copies:
        copy.start()
    for copy in copies:
        copy.wait()


def finish(groups, pieces, done):
    return pl.pallas_call(
        functools.partial(finish_kernel, groups),
        in_specs=[ANY] * (1 + len(pieces)),
        out_specs=ANY,
        out_shape=NEW_WEIGHT,
        scratch_shapes=[pltpu.SemaphoreType.DMA((count_copies(groups),))],
        input_output_aliases={len(pieces): 0},
        compiler_params=limit(1),
        name="finish",
    )(*pieces, done)


def swapped(array, axis, size, k):
    return lax.ppermute(array, axis, [(i, i ^ k) for i in range(size)])


def crossed(array, first, k):
    perm = []
    for i in range(32):
        y, c, x = i >> 3, (i >> 2) & 1, i & 3
        to = (y, c, x ^ k) if c == first else (y ^ k, c, x)
        perm.append((i, (to[0] << 3) | (to[1] << 2) | to[2]))
    return lax.ppermute(array, ("y", "c", "x"), perm)


def other_core(array):
    return swapped(array, "c", 2, 1)


def per_device(weight, momentum, grad, positions):
    table = jnp.asarray(basis_parts())
    sent = extract(momentum[0], grad[0], positions[0], table)
    arrived = lax.all_to_all(sent, ("zh", "y"), 0, 0, tiled=True)
    fresh, smooth = decode(begin(arrived), other_core(arrived), other_core(weight), other_core(table))
    fresh_z = swapped(fresh, "zl", 2, 1)
    near = join_near([fresh, smooth, other_core(smooth)])
    beside = [crossed(near, 0, k) for k in RING[:2]]
    across = crossed(join_four(near, fresh_z), 0, RING[2])
    firsts = [near, *beside, across]
    firsts_z = [fresh_z] + [crossed(fresh_z, 0, k) for k in RING[:2]]
    far = join_far(firsts + firsts_z)
    kept_state, token = kept(momentum[0], grad[0], sent, table, far)
    one, two, three = (crossed(far, 1, k) for k in RING)
    laid, new_weight = lay(firsts, token, [(0, (0, 1), (0,)), (1, (0, 1), (0,))], [far, one])
    direction, new_weight = choose(
        laid,
        other_core(laid),
        [(0, (0, 1), (1,)), (1, (0, 1), (1,)), (2, (0, 1), (0,)), (3, (0, 1), (0,))],
        [other_core(far), other_core(one), two, three],
        new_weight,
    )
    new_weight = finish(
        [(2, (0, 1), (1,)), (3, (0, 1), (1,))], [other_core(two), other_core(three)], new_weight
    )
    return (kept_state[None], direction, new_weight)


def solution(mesh):
    split = Mesh(mesh.devices.reshape(4, 4, 2, 4, 2), ("zh", "y", "c", "x", "zl"))
    in_specs = (
        P(None, SHARD),
        P(REPLICA, None, SHARD),
        P(REPLICA, None, SHARD),
        P(REPLICA, None, SHARD, None),
    )
    out_specs = (P(REPLICA, None, SHARD), P(None, SHARD), P())
    return jax.shard_map(
        per_device, mesh=split, in_specs=in_specs, out_specs=out_specs, check_vma=False
    )
```

```python
import functools
import math

import jax
import jax.numpy as jnp
import numpy as np
from jax import lax
from jax.experimental import pallas as pl
from jax.experimental.pallas import tpu as pltpu
from jax.sharding import Mesh
from jax.sharding import PartitionSpec as P

GROUP = 64
REPLICA = ("zh", "y", "c")
SHARD = ("x", "zl")
beta_decay = 0.9
step_rate = 0.02
F32, BF16 = jnp.float32, jnp.bfloat16
VMEM = pl.BlockSpec(memory_space=pltpu.VMEM)
RING = (3, 1, 2)
ANY = pl.BlockSpec(memory_space=pl.ANY)
HBM = pl.BlockSpec(memory_space=pltpu.HBM)


def limit(mib):
    return pltpu.CompilerParams(vmem_limit_bytes=int(mib * 2**20))


def basis_parts():
    freq, cells = np.arange(GROUP)[:, None], np.arange(GROUP)[None, :]
    scales = np.where(freq == 0, math.sqrt(1.0 / GROUP), math.sqrt(2.0 / GROUP))
    table = scales * np.cos(math.pi * (2.0 * cells + 1.0) * freq / (2.0 * GROUP))
    four = np.kron(np.eye(4), table)
    high = four.astype(jnp.bfloat16)
    low = (four - high.astype(np.float64)).astype(jnp.bfloat16)
    return np.stack([high, low, high.T, low.T])


def two_parts(value):
    high = value.astype(BF16)
    return high, (value - high.astype(F32)).astype(BF16)


def rows_by_rows(left, right):
    return lax.dot_general(left, right, (((1,), (1,)), ((), ())), preferred_element_type=F32)


def rows_by_cols(left, right):
    return lax.dot_general(left, right, (((1,), (0,)), ((), ())), preferred_element_type=F32)


def product(dot, left, right):
    lines = left[0].shape[0]
    both = dot(jnp.concatenate(left, axis=0), right[0])
    return both[:lines] + both[lines:] + dot(left[0], right[1])


def one_hot_rows(place, lines, dtype):
    line = lax.broadcasted_iota(jnp.int32, (lines, place.shape[1]), 0)
    return jnp.where(line == place, 1.0, 0.0).astype(dtype)


def split_place(flat):
    lane = lax.broadcasted_iota(jnp.int32, flat.shape, 1)
    return (flat >> 6) + ((lane >> 5) << 6), flat & 63


def spread(values, column):
    line = lax.broadcasted_iota(jnp.int32, (GROUP, values.shape[1]), 0)
    return two_parts(jnp.where(line == column, values, 0.0))


def extract_kernel(momentum, grad, positions, table, out, m_in, g_in, p_in, basis, places, sems):
    copies = []
    for half in range(2):
        columns = pl.ds(512 * half, 512)
        copies.append((momentum.at[:, columns], m_in.at[half]))
        copies.append((grad.at[:, columns], g_in.at[half]))
        if half == 0:
            copies.append((table, basis))
            copies.append((positions, p_in))
    copies = [pltpu.make_async_copy(*pair, sems.at[n]) for n, pair in enumerate(copies)]
    for copy in copies:
        copy.start()
    for half in range(2):
        for copy in copies[4:] if half else copies[:4]:
            copy.wait()
        if half == 0:
            for x in range(4):
                places[:, 32 * x : 32 * x + 32] = p_in[x]
        straight, turned = (basis[0], basis[1]), (basis[2], basis[3])
        moved = beta_decay * m_in[half] + g_in[half].astype(F32)
        moved = [two_parts(moved[:, 256 * g : 256 * g + 256]) for g in range(2)]
        rows = [two_parts(product(rows_by_rows, straight, value)) for value in moved]
        coeff = [two_parts(product(rows_by_cols, value, turned)) for value in rows]
        for g in range(2):
            lines = []
            for q in range(4):
                at = 8 * half + 4 * g + q
                flat = places[at : at + 1, :]
                row, column = split_place(flat)
                block = jnp.concatenate([part[GROUP * q : GROUP * (q + 1)] for part in coeff[g]], axis=0)
                found = rows_by_cols(block, one_hot_rows(row, 4 * GROUP, BF16))
                found = found[:GROUP] + found[GROUP:]
                line = lax.broadcasted_iota(jnp.int32, found.shape, 0)
                lines.append(jnp.sum(jnp.where(line == column, found, 0.0), axis=0, keepdims=True))
                lines.append(flat.astype(F32))
            tile = jnp.concatenate(lines, axis=0)
            for z in range(4):
                out[4 * z + 2 * half + g] = tile


def extract(momentum, grad, positions, table):
    return pl.pallas_call(
        extract_kernel,
        in_specs=[HBM] * 4,
        out_specs=VMEM,
        out_shape=jax.ShapeDtypeStruct((16, 8, 128), F32),
        scratch_shapes=[
            pltpu.VMEM((2, 256, 512), F32),
            pltpu.VMEM((2, 256, 512), BF16),
            pltpu.VMEM((4, 16, 32), jnp.int32),
            pltpu.VMEM((4, 256, 256), BF16),
            pltpu.VMEM((16, 128), jnp.int32),
            pltpu.SemaphoreType.DMA((6,)),
        ],
        cost_estimate=pl.CostEstimate(flops=10**9, bytes_accessed=2 * 2**20, transcendentals=0),
        compiler_params=limit(59),
        name="extract",
    )(momentum, grad, positions, table)


def kept_kernel(momentum, grad, sent, basis, far, out, token):
    straight, turned = (basis[0], basis[1]), (basis[2], basis[3])
    grids = []
    for g in range(2):
        tile, blocks = sent[g], []
        for q in range(4):
            row, column = split_place(tile[2 * q + 1 : 2 * q + 2].astype(jnp.int32))
            high, low = spread(tile[2 * q : 2 * q + 1], column)
            hot = one_hot_rows(row, 4 * GROUP, BF16)
            blocks.append(rows_by_rows(high, hot) + rows_by_rows(low, hot))
        grids.append(two_parts(jnp.concatenate(blocks, axis=0)))
    half = [two_parts(product(rows_by_rows, turned, grid)) for grid in grids]
    dense = [product(rows_by_cols, value, straight) for value in half]
    moved = beta_decay * momentum[...] + grad[...].astype(F32)
    for g in range(2):
        columns = slice(256 * g, 256 * g + 256)
        out[:, columns] = moved[:, columns] - dense[g]
    token[...] = jnp.zeros_like(token)


def kept(momentum, grad, sent, table, far):
    block = pl.BlockSpec((256, 512), lambda g: (0, g))
    whole = lambda *shape: pl.BlockSpec(shape, lambda g: (0,) * len(shape))
    return pl.pallas_call(
        kept_kernel,
        grid=(2,),
        in_specs=[block, block, pl.BlockSpec((2, 8, 128), lambda g: (g, 0, 0)), whole(4, 256, 256), ANY],
        out_specs=[block, whole(8, 128)],
        out_shape=[jax.ShapeDtypeStruct((256, 1024), F32), jax.ShapeDtypeStruct((8, 128), F32)],
        cost_estimate=pl.CostEstimate(flops=2 * 10**9, bytes_accessed=3 * 2**20, transcendentals=0),
        compiler_params=limit(12),
        name="kept",
    )(momentum, grad, sent, table, far)


def gather_entries(arrived, totals):
    core = lax.axis_index("c")
    tiles = []
    for source in range(16):
        tile = arrived[source]
        tiles.append(jnp.where(core == 0, tile[:4], tile[4:]))
    for pair in range(0, len(tiles), 2):
        for j in range(2):
            lefts, hots = [], []
            for tile in tiles[pair : pair + 2]:
                row, line = split_place(tile[2 * j + 1 : 2 * j + 2].astype(jnp.int32))
                lefts.append(jnp.concatenate(spread(tile[2 * j : 2 * j + 1], line), axis=0))
                hots.append(one_hot_rows(row, 4 * GROUP, BF16))
            found = rows_by_rows(jnp.concatenate(lefts, axis=1), jnp.concatenate(hots, axis=1))
            totals[j] = found if totals[j] is None else totals[j] + found
    return [total[:GROUP] + total[GROUP:] for total in totals]


def begin_kernel(arrived, out):
    for j, total in enumerate(gather_entries(arrived, [None, None])):
        out[GROUP * j : GROUP * (j + 1)] = total


def begin(arrived):
    return pl.pallas_call(
        begin_kernel,
        in_specs=[VMEM],
        out_specs=VMEM,
        out_shape=jax.ShapeDtypeStruct((2 * GROUP, 4 * GROUP), F32),
        cost_estimate=pl.CostEstimate(flops=10**9, bytes_accessed=2**20, transcendentals=0),
        compiler_params=limit(8),
        name="begin",
    )(arrived)


def decode_kernel(begun, arrived, weight, basis, fresh, smooth_out):
    place = pl.multiple_of((lax.axis_index("y") * 2 + lax.axis_index("c")) * 128, 128)
    blocks = gather_entries(arrived, [None, None])
    grid = two_parts(begun[...] + jnp.concatenate(blocks, axis=0))
    half = product(rows_by_rows, (basis[2], basis[3]), grid)
    dense = product(rows_by_cols, two_parts(half), (basis[0, :128, :128], basis[1, :128, :128]))
    smooth = jnp.tanh(dense)
    smooth_out[0] = smooth.astype(BF16)
    fresh[0] = (weight[:, pl.ds(place, 128)].astype(F32) - step_rate * smooth).astype(BF16)


def decode(begun, arrived, weight, table):
    return pl.pallas_call(
        decode_kernel,
        in_specs=[VMEM] * 4,
        out_specs=[VMEM] * 2,
        out_shape=[jax.ShapeDtypeStruct((1, 256, 128), BF16)] * 2,
        cost_estimate=pl.CostEstimate(flops=10**9, bytes_accessed=2**20, transcendentals=32768),
        compiler_params=limit(8),
        name="decode",
    )(begun, arrived, weight, table)


def near_kernel(a, b, c, out):
    for k, ref in enumerate((a, b, c)):
        out[k] = ref[0]


def join_near(arrays):
    return pl.pallas_call(
        near_kernel,
        in_specs=[VMEM] * 3,
        out_specs=VMEM,
        out_shape=jax.ShapeDtypeStruct((3, 256, 128), BF16),
        compiler_params=limit(4),
        name="join_near",
    )(*arrays)


def four_kernel(near, fresh_z, out):
    out[:3] = near[...]
    out[3] = fresh_z[0]


def join_four(near, fresh_z):
    return pl.pallas_call(
        four_kernel,
        in_specs=[VMEM] * 2,
        out_specs=VMEM,
        out_shape=jax.ShapeDtypeStruct((4, 256, 128), BF16),
        compiler_params=limit(4),
        name="join_four",
    )(near, fresh_z)


def far_kernel(a, b, c, across, a_z, b_z, c_z, out):
    for k, ref in enumerate((a, b, c, across, a_z, b_z, c_z)):
        out[k] = ref[0]
    out[7] = across[3]


def join_far(arrays):
    return pl.pallas_call(
        far_kernel,
        in_specs=[VMEM] * 7,
        out_specs=VMEM,
        out_shape=jax.ShapeDtypeStruct((8, 256, 128), BF16),
        compiler_params=limit(4),
        name="join_far",
    )(*arrays)


def piece_copies(groups, pieces, out, sems):
    core, x, y, zl = (lax.axis_index(name) for name in ("c", "x", "y", "zl"))
    copies = []
    at = 0
    for k2, zs, others in groups:
        for other in others:
            at_core = jnp.bitwise_xor(core, other)
            for i, dz in enumerate(zs):
                for k1 in range(4):
                    first, second = (0, *RING)[k1], (0, *RING)[k2]
                    dx = jnp.where(at_core == 0, first, second)
                    dy = jnp.where(at_core == 0, second, first)
                    shard = jnp.bitwise_xor(x, dx) * 2 + jnp.bitwise_xor(zl, dz)
                    tile = shard * 8 + jnp.bitwise_xor(y, dy) * 2 + at_core
                    columns = pl.ds(pl.multiple_of(tile * 128, 128), 128)
                    copies.append(
                        pltpu.make_async_copy(
                            pieces[at].at[4 * i + k1], out.at[:, columns], sems.at[len(copies)]
                        )
                    )
            at += 1
    return copies


def count_copies(groups):
    return sum(4 * len(zs) * len(others) for _, zs, others in groups)


NEW_WEIGHT = jax.ShapeDtypeStruct((256, 8192), BF16)
LAID = jax.ShapeDtypeStruct((256, 1024), BF16)


def lay_kernel(groups, *refs):
    firsts, pieces, (laid, out, sems) = refs[:4], refs[5:-3], refs[-3:]
    copies = piece_copies(groups, pieces, out, sems)
    for copy in copies:
        copy.start()
    core, y = lax.axis_index("c"), lax.axis_index("y")
    for k in range(4):
        for other in range(2):
            tile = jnp.bitwise_xor(y, (0, *RING)[k]) * 2 + jnp.bitwise_xor(core, other)
            laid[:, pl.ds(pl.multiple_of(tile * 128, 128), 128)] = firsts[k][1 + other]
    for copy in copies:
        copy.wait()


def lay(firsts, token, groups, pieces):
    return pl.pallas_call(
        functools.partial(lay_kernel, groups),
        in_specs=[VMEM] * 4 + [ANY] * (1 + len(pieces)),
        out_specs=[VMEM, ANY],
        out_shape=[LAID, NEW_WEIGHT],
        scratch_shapes=[pltpu.SemaphoreType.DMA((count_copies(groups),))],
        compiler_params=limit(4),
        name="lay",
    )(*firsts, token, *pieces)


def choose_kernel(groups, mine, theirs, *refs):
    pieces, (direction, out, sems, sem) = refs[:-5], refs[-4:]
    copies = piece_copies(groups, pieces, out, sems)
    for copy in copies:
        copy.start()
    for core, source in enumerate((theirs, mine)):

        @pl.when(lax.axis_index("c") == core)
        def _():
            copy = pltpu.make_async_copy(source, direction, sem)
            copy.start()
            copy.wait()

    for copy in copies:
        copy.wait()


def choose(mine, theirs, groups, pieces, done):
    return pl.pallas_call(
        functools.partial(choose_kernel, groups),
        in_specs=[ANY] * (3 + len(pieces)),
        out_specs=[ANY] * 2,
        out_shape=[LAID, NEW_WEIGHT],
        scratch_shapes=[pltpu.SemaphoreType.DMA((count_copies(groups),)), pltpu.SemaphoreType.DMA],
        input_output_aliases={2 + len(pieces): 1},
        compiler_params=limit(1),
        name="choose",
    )(mine, theirs, *pieces, done)


def finish_kernel(groups, *refs):
    pieces, (out, sems) = refs[:-3], refs[-2:]
    copies = piece_copies(groups, pieces, out, sems)
    for copy in copies:
        copy.start()
    for copy in copies:
        copy.wait()


def finish(groups, pieces, done):
    return pl.pallas_call(
        functools.partial(finish_kernel, groups),
        in_specs=[ANY] * (1 + len(pieces)),
        out_specs=ANY,
        out_shape=NEW_WEIGHT,
        scratch_shapes=[pltpu.SemaphoreType.DMA((count_copies(groups),))],
        input_output_aliases={len(pieces): 0},
        compiler_params=limit(1),
        name="finish",
    )(*pieces, done)


def swapped(array, axis, size, k):
    return lax.ppermute(array, axis, [(i, i ^ k) for i in range(size)])


def crossed(array, first, k):
    perm = []
    for i in range(32):
        y, c, x = i >> 3, (i >> 2) & 1, i & 3
        to = (y, c, x ^ k) if c == first else (y ^ k, c, x)
        perm.append((i, (to[0] << 3) | (to[1] << 2) | to[2]))
    return lax.ppermute(array, ("y", "c", "x"), perm)


def other_core(array):
    return swapped(array, "c", 2, 1)


def per_device(weight, momentum, grad, positions):
    table = jnp.asarray(basis_parts())
    sent = extract(momentum[0], grad[0], positions[0], table)
    arrived = lax.all_to_all(sent, ("zh", "y"), 0, 0, tiled=True)
    fresh, smooth = decode(begin(arrived), other_core(arrived), other_core(weight), other_core(table))
    fresh_z = swapped(fresh, "zl", 2, 1)
    near = join_near([fresh, smooth, other_core(smooth)])
    beside = [crossed(near, 0, k) for k in RING[:2]]
    across = crossed(join_four(near, fresh_z), 0, RING[2])
    firsts = [near, *beside, across]
    firsts_z = [fresh_z] + [crossed(fresh_z, 0, k) for k in RING[:2]]
    far = join_far(firsts + firsts_z)
    kept_state, token = kept(momentum[0], grad[0], sent, table, far)
    one, two, three = (crossed(far, 1, k) for k in RING)
    laid, new_weight = lay(firsts, token, [(0, (0, 1), (0,)), (1, (0, 1), (0,))], [far, one])
    direction, new_weight = choose(
        laid,
        other_core(laid),
        [(0, (0, 1), (1,)), (1, (0, 1), (1,)), (2, (0, 1), (0,)), (3, (0, 1), (0,))],
        [other_core(far), other_core(one), two, three],
        new_weight,
    )
    new_weight = finish(
        [(2, (0, 1), (1,)), (3, (0, 1), (1,))], [other_core(two), other_core(three)], new_weight
    )
    return (kept_state[None], direction, new_weight)


def solution(mesh):
    split = Mesh(mesh.devices.reshape(4, 4, 2, 4, 2), ("zh", "y", "c", "x", "zl"))
    in_specs = (
        P(None, SHARD),
        P(REPLICA, None, SHARD),
        P(REPLICA, None, SHARD),
        P(REPLICA, None, SHARD, None),
    )
    out_specs = (P(REPLICA, None, SHARD), P(None, SHARD), P())
    return jax.shard_map(
        per_device, mesh=split, in_specs=in_specs, out_specs=out_specs, check_vma=False
    )
```
